128 devices in a mesh: dp: 4 (over y_hi, core), context: 32 (over z, x, y_lo).
Axes of the slice: x: 4, y: 4 (y_hi: 2, y_lo: 2; y = y_hi * 2 + y_lo), z: 4, core: 2. Of those that a mesh axis runs over, the one named last changes fastest.
Arguments:
- tokens: bfloat16 [4096, 8192], P('context', 'dp'), may hold values from -6 to 6
- in_weight: bfloat16 [8192, 2, 2048], P(None, None, 'dp'), may hold values from -0.0625 to 0.0625
- short_taps: float32 [2, 3, 2048], P(None, None, 'dp'), may hold values from -1 to 1
- filters: float32 [2048, 4096], P(('dp', 'context')), may hold values from -1 to 1, as said below
- cotangent: bfloat16 [2048, 4096], P('dp', 'context'), may hold values from -1.5 to 1.5
Outputs:
- gated_out: bfloat16 [2048, 4096], P('dp', 'context')
- token_grad: bfloat16 [4096, 8192], P('context', 'dp')
- weight_grad: bfloat16 [8192, 2, 2048], P('context', None, 'dp')
- filter_grad: float32 [2048, 4096], P(('dp', 'context'))
The draws below stay inside these ranges and needn't reach their ends.
Inputs may be any that keep to these rules, and one draw needn't show every extreme that they name: `filters`: each channel's filter is a rough sequence times a decay over the lags.
All inputs are finite; a program needn't handle non-finite values.
Results may differ from the reference program's by a relative error of at most 0.013.
Values may be sent and summed in bfloat16 or wider, within the bound.
A program may use at most 128 MiB of HBM per device.

```python
import jax
import jax.numpy as jnp

D = 8192
C = 2048
SEQ = 4096
N_DP = 4


def draw_filters(key, part):
    key = jax.random.fold_in(key, 7)
    rate_key, noise_key = jax.random.split(key)
    position = jnp.arange(SEQ).astype(jnp.float32)[None, :]
    noise = jnp.clip(jax.random.normal(noise_key, (C, SEQ), jnp.float32), -3.0, 3.0)
    low = jnp.log(1.0 / (2.0 * SEQ))
    rate = jnp.exp(jax.random.uniform(rate_key, (C, 1), jnp.float32, low, jnp.log(1.0 / 32.0)))
    amplitude = jnp.sqrt(2.0 * rate)
    return amplitude * jnp.exp(-rate * position) * noise


def spiked(values, own_key, source, target, shards_of, factor):
    def block_of(dim):
        return (jnp.arange(values.shape[dim]) // (values.shape[dim] // shards_of)).reshape((-1,) + (1,) * (values.ndim - 1 - dim))

    one_side = jax.random.permutation(own_key, shards_of)[block_of(target)]
    far = (block_of(target) + shards_of // 2) % shards_of
    return jnp.where((block_of(source) == one_side) | (block_of(source) == far), factor * values, values)


def shard_levels(stream_key, extent, shards, low, top_value):
    def one(dim, parts):
        steps = jax.random.uniform(jax.random.fold_in(jax.random.fold_in(stream_key, 6), dim), (parts,), jnp.float32, low / len(shards), top_value / len(shards))
        return jnp.repeat(jnp.exp(steps), extent[dim] // parts).reshape((-1,) + (1,) * (len(extent) - dim - 1))

    gain = one(*shards[0])
    for cut in shards[1:]:
        gain = gain * one(*cut)
    return gain


def gaussian(rng, shape, deviation, reach, cuts=(), kind=jnp.bfloat16):
    gain = shard_levels(rng, shape, cuts, -0.22, 0.18) if cuts else 1.0
    entries = jax.random.normal(rng, shape, jnp.float32) * deviation * gain
    return jnp.minimum(jnp.maximum(entries, -reach), reach).astype(kind)


def bell_draw_with(own_key, extent, deviation, bound, pieces, heavy, dtype=jnp.bfloat16):
    drawn = deviation * jax.random.normal(own_key, extent, jnp.float32)
    if pieces:
        drawn = drawn * shard_levels(own_key, extent, pieces, -0.22, 0.18)
    return jnp.clip(spiked(drawn, jax.random.fold_in(own_key, 3), *heavy), -bound, bound).astype(dtype)


def setup_inputs(seed: int = 0) -> dict:
    arg_keys = jax.random.split(jax.random.key(seed), 6)
    tokens = bell_draw_with(arg_keys[0], (SEQ, D), 1.0, 6.0, ((0, 32), (1, 4)), (0, 1, 32, 2.75))
    in_weight = gaussian(arg_keys[1], (D, 2, C), D ** -0.5, 0.0625, ((2, 4),))
    short_taps = jnp.clip(jax.random.uniform(arg_keys[2], (2, 3, C), jnp.float32, -1.0, 1.0) * shard_levels(arg_keys[2], (2, 3, C), ((2, 4),), -0.4, 0.0), -1.0, 1.0)
    filters = draw_filters(jax.random.fold_in(arg_keys[5], 71), 0)
    cotangent = gaussian(arg_keys[4], (C, SEQ), 0.25, 1.5, ((0, 4), (1, 32)))
    return {"tokens": tokens, "in_weight": in_weight, "short_taps": short_taps, "filters": filters, "cotangent": cotangent}


def short_forward(projected, short_taps):
    length = projected.shape[2]
    padded = jnp.pad(projected, ((0, 0), (0, 0), (2, 0)))
    total = jnp.zeros_like(projected)
    for offset in range(3):
        total = total + short_taps[:, offset, :, None] * padded[:, :, 2 - offset:2 - offset + length]
    return total


def short_backward(grads, short_taps):
    length = grads.shape[2]
    padded = jnp.pad(grads, ((0, 0), (0, 0), (0, 2)))
    total = jnp.zeros_like(grads)
    for offset in range(3):
        total = total + short_taps[:, offset, :, None] * padded[:, :, offset:offset + length]
    return total


def reference(tokens, in_weight, short_taps, filters, cotangent):
    length = SEQ
    total = 2 * length
    tokens_wide = tokens.astype(jnp.float32)
    weight_wide = in_weight.astype(jnp.float32)
    projected = jnp.einsum('td,dkc->kct', tokens_wide, weight_wide)
    streams = short_forward(projected, short_taps)
    gate = streams[0]
    value = streams[1]
    filt_freq = jnp.fft.rfft(filters, total, axis=1)
    value_freq = jnp.fft.rfft(value, total, axis=1)
    filtered = jnp.fft.irfft(filt_freq * value_freq, total, axis=1)[:, :length]
    gated_out = (gate * filtered).astype(jnp.bfloat16)
    grad_in = cotangent.astype(jnp.float32)
    grad_gate = grad_in * filtered
    grad_filtered = grad_in * gate
    grad_freq = jnp.fft.rfft(grad_filtered, total, axis=1)
    grad_value = jnp.fft.irfft(jnp.conj(filt_freq) * grad_freq, total, axis=1)[:, :length]
    filter_grad = jnp.fft.irfft(jnp.conj(value_freq) * grad_freq, total, axis=1)[:, :length]
    grad_streams = jnp.stack([grad_gate, grad_value])
    proj_grad = short_backward(grad_streams, short_taps).astype(jnp.bfloat16)
    proj_wide = proj_grad.astype(jnp.float32)
    slab = C // N_DP
    token_grad = jnp.zeros((length, D), jnp.float32)
    for group in range(N_DP):
        part_grad = proj_wide[:, group * slab:(group + 1) * slab, :]
        part_weight = weight_wide[:, :, group * slab:(group + 1) * slab]
        partial_value = jnp.einsum('kct,dkc->td', part_grad, part_weight)
        token_grad = token_grad + partial_value.astype(jnp.bfloat16).astype(jnp.float32)
    weight_grad = jnp.einsum('td,kct->dkc', tokens_wide, proj_wide)
    return gated_out, token_grad.astype(jnp.bfloat16), weight_grad.astype(jnp.bfloat16), filter_grad
```

```python
import functools
import math

import jax
import jax.numpy as jnp
import numpy as np
from jax import lax
from jax.experimental import pallas as pl
from jax.experimental.pallas import tpu as pltpu
from jax.sharding import PartitionSpec as P

OUTER = 64
INNER = 128
TOTAL = OUTER * INNER
HALF = OUTER // 2
KEPT = [0, 8, 16, 24, 32] + [k1 + 8 * k2 for k1 in (1, 2, 3) for k2 in range(8)] + [4, 12, 20, 28]
ROWS = len(KEPT)


def add(a, b):
    return b if a is None else a if b is None else a + b


def neg(a):
    return None if a is None else -a


def sub(a, b):
    return a if b is None else neg(b) if a is None else a - b


def scaled(a, factor):
    if a is None or abs(factor) < 1e-12:
        return None
    if abs(factor - 1) < 1e-12:
        return a
    if abs(factor + 1) < 1e-12:
        return -a
    return a * np.float32(factor)


def cadd(a, b):
    return (add(a[0], b[0]), add(a[1], b[1]))


def csub(a, b):
    return (sub(a[0], b[0]), sub(a[1], b[1]))


def turned(a, step, count):
    step %= count
    if (8 * step) % count == 0 and (8 * step // count) % 2 == 1:
        eighth = 8 * step // count
        root = math.sqrt(0.5)
        re, im = a
        if eighth == 1:
            pair = (sub(re, im), add(re, im))
        elif eighth == 3:
            pair = (neg(add(re, im)), sub(re, im))
        elif eighth == 5:
            pair = (sub(im, re), neg(add(re, im)))
        else:
            pair = (add(re, im), sub(im, re))
        return (scaled(pair[0], root), scaled(pair[1], root))
    angle = 2 * math.pi * step / count
    cos, sin = math.cos(angle), math.sin(angle)
    return (
        sub(scaled(a[0], cos), scaled(a[1], sin)),
        add(scaled(a[0], sin), scaled(a[1], cos)),
    )


def dft(values, sign):
    count = len(values)
    if count == 1:
        return values
    even = dft(values[0::2], sign)
    odd = dft(values[1::2], sign)
    odd = [turned(entry, sign * index, count) for index, entry in enumerate(odd)]
    return [cadd(a, b) for a, b in zip(even, odd)] + [csub(a, b) for a, b in zip(even, odd)]


def outer_forward(load):
    parts = []
    for second in range(8):
        line = [(load(8 * first + second), None) if first < 4 else (None, None) for first in range(8)]
        parts.append(dft(line, -1)[:5])
    results = []
    for first in (0, 1, 2, 3, 4):
        line = [turned(parts[second][first], -second * first, OUTER) for second in range(8)]
        full = dft(line, -1)
        results += {0: full[:5], 4: full[:4]}.get(first, full)
    return results


def real_sum(values, index):
    total = None
    for j, entry in enumerate(values):
        total = add(total, turned(entry, j * index, 8)[0])
    return total


def real_line(values, count):
    top = values[0][0]
    last = values[4][0]
    a = add(top, last)
    b = sub(top, last)
    (r1, i1), (r2, i2), (r3, i3) = values[1:4]
    s13, d13 = add(r1, r3), sub(r1, r3)
    si, di = add(i1, i3), sub(i1, i3)
    root = math.sqrt(0.5)
    p = scaled(sub(d13, si), root)
    q = scaled(add(d13, si), root)
    out = [
        add(add(a, r2), s13),
        add(sub(b, i2), p),
        sub(sub(a, r2), di),
        sub(add(b, i2), q),
    ]
    if count > 4:
        out += [
            sub(add(a, r2), s13),
            sub(sub(b, i2), p),
            add(sub(a, r2), di),
            add(add(b, i2), q),
        ]
    return out


def outer_inverse(load):
    zero = real_line([load(row) for row in range(5)], 8)
    lines = []
    for first in (1, 2, 3):
        line = dft([load(5 + 8 * (first - 1) + second) for second in range(8)], 1)
        lines.append([turned(line[second], second * first, OUTER) for second in range(8)])
    tail = dft([load(29 + second) if second < 4 else (None, None) for second in range(8)], 1)
    tail = [turned(tail[second], second, 16)[0] for second in range(8)]
    results = [None] * HALF
    for second in range(8):
        line = [(zero[second], None)] + [lines[first][second] for first in range(3)] + [(tail[second], None)]
        for first, entry in enumerate(real_line(line, 4)):
            results[8 * first + second] = entry
    return results


def tables():
    index = np.arange(INNER, dtype=np.float64)
    angle = 2 * np.pi / INNER * (np.outer(index, index) % INNER)
    cos, sin = np.cos(angle), np.sin(angle)
    wide = np.block([[cos, -sin], [sin, cos]])
    high = wide.astype(jnp.bfloat16)
    low = (wide - high.astype(np.float64)).astype(jnp.bfloat16)
    inverse = wide.T
    inverse_high = inverse.astype(jnp.bfloat16)
    inverse_low = (inverse - inverse_high.astype(np.float64)).astype(jnp.bfloat16)
    matrices = np.stack([high, low, inverse_high, inverse_low])
    turn = 2 * np.pi / TOTAL * np.outer(np.array(KEPT, np.float64), index)
    weight = np.array([1.0 if k in (0, HALF) else 2.0 for k in KEPT])[:, None] / TOTAL
    turns = np.stack([np.cos(turn), np.sin(turn), weight * np.cos(turn), weight * np.sin(turn)])
    return matrices, turns.astype(np.float32)


def times_matrix(wide, high, low):
    top = wide.astype(jnp.bfloat16)
    rest = (wide - top.astype(jnp.float32)).astype(jnp.bfloat16)
    dot = functools.partial(jnp.dot, preferred_element_type=jnp.float32)
    return dot(top, high) + (dot(rest, high) + dot(top, low))


def lagged(here, before, lag):
    lane = lax.broadcasted_iota(jnp.int32, here.shape, here.ndim - 1)
    rolled = pltpu.roll(here, lag, here.ndim - 1)
    if before is None:
        return jnp.where(lane < lag, 0.0, rolled)
    return jnp.where(lane < lag, pltpu.roll(before, lag, here.ndim - 1), rolled)


def led(here, after, lead):
    lane = lax.broadcasted_iota(jnp.int32, here.shape, here.ndim - 1)
    width = here.shape[-1]
    rolled = pltpu.roll(here, width - lead, here.ndim - 1)
    if after is None:
        return jnp.where(lane >= width - lead, 0.0, rolled)
    return jnp.where(lane >= width - lead, pltpu.roll(after, width - lead, here.ndim - 1), rolled)


def conv_kernel(
    proj_ref, cot_ref, filt_ref, taps_ref, mat_ref, turn_ref,
    back_ref, pair_ref, fgrad_ref,
    gate_ref, value_ref, gfilt_ref, gval_ref, spec_ref, prod_ref,
):
    channels = filt_ref.shape[0]

    def short(stream, n):
        here = proj_ref[n, stream].astype(jnp.float32)
        before = proj_ref[n - 1, stream].astype(jnp.float32) if n else None
        total = taps_ref[stream, 0] * here
        for lag in (1, 2):
            total = total + taps_ref[stream, lag] * lagged(here, before, lag)
        return total

    for n in range(HALF):
        gate = short(0, n)
        gate_ref[n] = gate
        gfilt_ref[n] = cot_ref[n].astype(jnp.float32) * gate
        value_ref[n] = short(1, n)

    sources = (
        lambda n: filt_ref[:, n * INNER : (n + 1) * INNER],
        lambda n: value_ref[n],
        lambda n: gfilt_ref[n],
    )
    for which, load in enumerate(sources):
        for row, (re, im) in enumerate(outer_forward(load)):
            cos = turn_ref[0, row][None, :]
            sin = turn_ref[1, row][None, :]
            at = pl.ds((which * ROWS + row) * channels, channels)
            if im is None:
                spec_ref[at, :INNER] = re * cos
                spec_ref[at, INNER:] = -(re * sin)
            else:
                spec_ref[at, :INNER] = re * cos + im * sin
                spec_ref[at, INNER:] = im * cos - re * sin
    size = ROWS * channels
    for which in range(3):
        at = pl.ds(which * size, size)
        spec_ref[at, :] = times_matrix(spec_ref[at, :], mat_ref[0], mat_ref[1])

    @pl.loop(0, ROWS)
    def _(row):
        def part(which):
            at = pl.ds(pl.multiple_of((which * ROWS + row) * channels, channels), channels)
            return spec_ref[at, :INNER], spec_ref[at, INNER:]

        (hr, hi), (vr, vi), (gr, gi) = part(0), part(1), part(2)

        def put(which, re, im):
            at = pl.ds(pl.multiple_of((which * ROWS + row) * channels, channels), channels)
            prod_ref[at, :INNER] = re
            prod_ref[at, INNER:] = im

        put(0, hr * vr - hi * vi, hr * vi + hi * vr)
        put(1, hr * gr + hi * gi, hr * gi - hi * gr)
        put(2, vr * gr + vi * gi, vr * gi - vi * gr)

    for which in range(3):
        at = pl.ds(which * size, size)
        prod_ref[at, :] = times_matrix(prod_ref[at, :], mat_ref[2], mat_ref[3])

    def turned_row(which):
        def load(row):
            cos = turn_ref[2, row][None, :]
            sin = turn_ref[3, row][None, :]
            at = pl.ds((which * ROWS + row) * channels, channels)
            re, im = prod_ref[at, :INNER], prod_ref[at, INNER:]
            return re * cos - im * sin, im * cos + re * sin

        return load

    for n, entry in enumerate(outer_inverse(turned_row(0))):
        back_ref[n, 2] = (gate_ref[n] * entry).astype(back_ref.dtype)
        gate_ref[n] = cot_ref[n].astype(jnp.float32) * entry
    for n, entry in enumerate(outer_inverse(turned_row(1))):
        gval_ref[n] = entry
    for n, entry in enumerate(outer_inverse(turned_row(2))):
        fgrad_ref[:, n * INNER : (n + 1) * INNER] = entry

    for stream, ref in enumerate((gate_ref, gval_ref)):
        for n in range(HALF):
            here = ref[n]
            after = ref[n + 1] if n + 1 < HALF else None
            total = taps_ref[stream, 0] * here
            for lead in (1, 2):
                total = total + taps_ref[stream, lead] * led(here, after, lead)
            total = total.astype(jnp.bfloat16)
            back_ref[n, stream] = total
            pair_ref[stream, :, n * INNER : (n + 1) * INNER] = total


def convolved(projected, cotangent, filters, taps):
    channels, length = filters.shape
    matrices, turns = tables()
    f32 = functools.partial(pltpu.VMEM, dtype=jnp.float32)
    return pl.pallas_call(
        conv_kernel,
        out_shape=(
            jax.ShapeDtypeStruct((HALF, 3, channels, INNER), jnp.bfloat16),
            jax.ShapeDtypeStruct((2, channels, length), jnp.bfloat16),
            jax.ShapeDtypeStruct((channels, length), jnp.float32),
        ),
        in_specs=[pl.BlockSpec(memory_space=pltpu.VMEM)] * 6,
        out_specs=[pl.BlockSpec(memory_space=pltpu.VMEM)] * 3,
        scratch_shapes=[
            f32((HALF, channels, INNER)),
            f32((HALF, channels, INNER)),
            f32((HALF, channels, INNER)),
            f32((HALF, channels, INNER)),
            f32((3 * ROWS * channels, 2 * INNER)),
            f32((3 * ROWS * channels, 2 * INNER)),
        ],
        compiler_params=pltpu.CompilerParams(vmem_limit_bytes=32 * 1024 * 1024),
        cost_estimate=pl.CostEstimate(flops=1_300_000_000, bytes_accessed=2_000_000, transcendentals=0),
        name="long_convolutions",
    )(projected, cotangent, filters, taps, jnp.asarray(matrices), jnp.asarray(turns))


def on_device(tokens, in_weight, short_taps, filters, cotangent):
    channels, length = filters.shape
    groups = lax.axis_size("context")
    rows = tokens.shape[0]
    slab = in_weight.shape[2]
    gathered = lax.all_gather(tokens, "dp", axis=1, tiled=True)
    cot_group = lax.all_to_all(
        cotangent.reshape(groups, channels, rows), "context", split_axis=0, concat_axis=0, tiled=True
    )
    projected = jnp.einsum("td,dkc->kct", gathered, in_weight, preferred_element_type=jnp.float32)
    outgoing = projected.astype(jnp.bfloat16).reshape(2, groups, channels, rows).transpose(1, 0, 2, 3)
    proj_group = lax.all_to_all(outgoing, "context", split_axis=0, concat_axis=0, tiled=True)
    own = lax.dynamic_slice_in_dim(short_taps, lax.axis_index("context") * channels, channels, axis=2)
    taps = jnp.broadcast_to(own[..., None], own.shape + (INNER,))
    back, pair, filter_grad = convolved(proj_group, cot_group, filters, taps)
    back = lax.all_to_all(back, "context", split_axis=0, concat_axis=0, tiled=True)
    gated_out = back[:, 2].reshape(slab, rows)
    proj_grad = back[:, :2].transpose(1, 0, 2, 3).reshape(2, slab, rows)
    partial_value = jnp.einsum("kct,dkc->td", proj_grad, in_weight, preferred_element_type=jnp.float32)
    token_grad = lax.psum_scatter(
        partial_value.astype(jnp.bfloat16), "dp", scatter_dimension=1, tiled=True
    )
    tokens_own = lax.all_to_all(gathered, "context", split_axis=1, concat_axis=0, tiled=True)
    whole = lax.all_gather(pair, "context", axis=0, tiled=False)
    weight_grad = jnp.einsum("td,gkct->dkgc", tokens_own, whole, preferred_element_type=jnp.float32)
    weight_grad = weight_grad.astype(jnp.bfloat16).reshape(tokens_own.shape[1], 2, slab)
    return (gated_out, token_grad, weight_grad, filter_grad)


def solution(mesh):
    placed = (
        P("context", "dp"),
        P(None, None, "dp"),
        P(None, None, "dp"),
        P(("dp", "context"), None),
        P("dp", "context"),
    )
    return jax.shard_map(
        on_device,
        mesh=mesh,
        in_specs=placed,
        out_specs=(
            P("dp", "context"),
            P("context", "dp"),
            P("context", None, "dp"),
            P(("dp", "context"), None),
        ),
        check_vma=False,
    )
```

```python
import functools
import math

import jax
import jax.numpy as jnp
import numpy as np
from jax import lax
from jax.experimental import pallas as pl
from jax.experimental.pallas import tpu as pltpu
from jax.sharding import PartitionSpec as P

OUTER = 64
INNER = 128
TOTAL = OUTER * INNER
HALF = OUTER // 2
KEPT = [0, 8, 16, 24, 32] + [k1 + 8 * k2 for k1 in (1, 2, 3) for k2 in range(8)] + [4, 12, 20, 28]
ROWS = len(KEPT)


def add(a, b):
    return b if a is None else a if b is None else a + b


def neg(a):
    return None if a is None else -a


def sub(a, b):
    return a if b is None else neg(b) if a is None else a - b


def scaled(a, factor):
    if a is None or abs(factor) < 1e-12:
        return None
    if abs(factor - 1) < 1e-12:
        return a
    if abs(factor + 1) < 1e-12:
        return -a
    return a * np.float32(factor)


def cadd(a, b):
    return (add(a[0], b[0]), add(a[1], b[1]))


def csub(a, b):
    return (sub(a[0], b[0]), sub(a[1], b[1]))


def turned(a, step, count):
    step %= count
    if (8 * step) % count == 0 and (8 * step // count) % 2 == 1:
        eighth = 8 * step // count
        root = math.sqrt(0.5)
        re, im = a
        if eighth == 1:
            pair = (sub(re, im), add(re, im))
        elif eighth == 3:
            pair = (neg(add(re, im)), sub(re, im))
        elif eighth == 5:
            pair = (sub(im, re), neg(add(re, im)))
        else:
            pair = (add(re, im), sub(im, re))
        return (scaled(pair[0], root), scaled(pair[1], root))
    angle = 2 * math.pi * step / count
    cos, sin = math.cos(angle), math.sin(angle)
    return (
        sub(scaled(a[0], cos), scaled(a[1], sin)),
        add(scaled(a[0], sin), scaled(a[1], cos)),
    )


def dft(values, sign):
    count = len(values)
    if count == 1:
        return values
    even = dft(values[0::2], sign)
    odd = dft(values[1::2], sign)
    odd = [turned(entry, sign * index, count) for index, entry in enumerate(odd)]
    return [cadd(a, b) for a, b in zip(even, odd)] + [csub(a, b) for a, b in zip(even, odd)]


def outer_forward(load):
    parts = []
    for second in range(8):
        line = [(load(8 * first + second), None) if first < 4 else (None, None) for first in range(8)]
        parts.append(dft(line, -1)[:5])
    results = []
    for first in (0, 1, 2, 3, 4):
        line = [turned(parts[second][first], -second * first, OUTER) for second in range(8)]
        full = dft(line, -1)
        results += {0: full[:5], 4: full[:4]}.get(first, full)
    return results


def real_line(values, count):
    top = values[0][0]
    last = values[4][0]
    a = add(top, last)
    b = sub(top, last)
    (r1, i1), (r2, i2), (r3, i3) = values[1:4]
    s13, d13 = add(r1, r3), sub(r1, r3)
    si, di = add(i1, i3), sub(i1, i3)
    root = math.sqrt(0.5)
    p = scaled(sub(d13, si), root)
    q = scaled(add(d13, si), root)
    out = [
        add(add(a, r2), s13),
        add(sub(b, i2), p),
        sub(sub(a, r2), di),
        sub(add(b, i2), q),
    ]
    if count > 4:
        out += [
            sub(add(a, r2), s13),
            sub(sub(b, i2), p),
            add(sub(a, r2), di),
            add(add(b, i2), q),
        ]
    return out


def outer_inverse(load):
    zero = real_line([load(row) for row in range(5)], 8)
    lines = []
    for first in (1, 2, 3):
        line = dft([load(5 + 8 * (first - 1) + second) for second in range(8)], 1)
        lines.append([turned(line[second], second * first, OUTER) for second in range(8)])
    tail = dft([load(29 + second) if second < 4 else (None, None) for second in range(8)], 1)
    tail = [turned(tail[second], second, 16)[0] for second in range(8)]
    results = [None] * HALF
    for second in range(8):
        line = [(zero[second], None)] + [lines[first][second] for first in range(3)] + [(tail[second], None)]
        for first, entry in enumerate(real_line(line, 4)):
            results[8 * first + second] = entry
    return results


def tables():
    index = np.arange(INNER, dtype=np.float64)
    angle = 2 * np.pi / INNER * (np.outer(index, index) % INNER)
    cos, sin = np.cos(angle), np.sin(angle)
    wide = np.block([[cos, -sin], [sin, cos]])
    high = wide.astype(jnp.bfloat16)
    low = (wide - high.astype(np.float64)).astype(jnp.bfloat16)
    inverse = wide.T
    inverse_high = inverse.astype(jnp.bfloat16)
    inverse_low = (inverse - inverse_high.astype(np.float64)).astype(jnp.bfloat16)
    matrices = np.stack([high, low, inverse_high, inverse_low])
    turn = 2 * np.pi / TOTAL * np.outer(np.array(KEPT, np.float64), index)
    weight = np.array([1.0 if k in (0, HALF) else 2.0 for k in KEPT])[:, None] / TOTAL
    turns = np.stack([np.cos(turn), np.sin(turn), weight * np.cos(turn), weight * np.sin(turn)])
    return matrices, turns.astype(np.float32)


def times_matrix(wide, high, low):
    top = wide.astype(jnp.bfloat16)
    rest = (wide - top.astype(jnp.float32)).astype(jnp.bfloat16)
    dot = functools.partial(jnp.dot, preferred_element_type=jnp.float32)
    return dot(top, high) + (dot(rest, high) + dot(top, low))


def lagged(here, before, lag):
    lane = lax.broadcasted_iota(jnp.int32, here.shape, here.ndim - 1)
    rolled = pltpu.roll(here, lag, here.ndim - 1)
    if before is None:
        return jnp.where(lane < lag, 0.0, rolled)
    return jnp.where(lane < lag, pltpu.roll(before, lag, here.ndim - 1), rolled)


def led(here, after, lead):
    lane = lax.broadcasted_iota(jnp.int32, here.shape, here.ndim - 1)
    width = here.shape[-1]
    rolled = pltpu.roll(here, width - lead, here.ndim - 1)
    if after is None:
        return jnp.where(lane >= width - lead, 0.0, rolled)
    return jnp.where(lane >= width - lead, pltpu.roll(after, width - lead, here.ndim - 1), rolled)


def conv_kernel(
    proj_ref, cot_ref, filt_ref, taps_ref, mat_ref, turn_ref,
    back_ref, fgrad_ref,
    gate_ref, value_ref, gfilt_ref, gval_ref, spec_ref, prod_ref,
):
    channels = filt_ref.shape[0]

    def short(stream, n):
        here = proj_ref[n, stream].astype(jnp.float32)
        before = proj_ref[n - 1, stream].astype(jnp.float32) if n else None
        total = taps_ref[stream, 0] * here
        for lag in (1, 2):
            total = total + taps_ref[stream, lag] * lagged(here, before, lag)
        return total

    for n in range(HALF):
        gate = short(0, n)
        gate_ref[n] = gate
        gfilt_ref[n] = cot_ref[n].astype(jnp.float32) * gate
        value_ref[n] = short(1, n)

    sources = (
        lambda n: filt_ref[:, n * INNER : (n + 1) * INNER],
        lambda n: value_ref[n],
        lambda n: gfilt_ref[n],
    )
    for which, load in enumerate(sources):
        for row, (re, im) in enumerate(outer_forward(load)):
            cos = turn_ref[0, row][None, :]
            sin = turn_ref[1, row][None, :]
            at = pl.ds((which * ROWS + row) * channels, channels)
            if im is None:
                spec_ref[at, :INNER] = re * cos
                spec_ref[at, INNER:] = -(re * sin)
            else:
                spec_ref[at, :INNER] = re * cos + im * sin
                spec_ref[at, INNER:] = im * cos - re * sin
    size = ROWS * channels
    for which in range(3):
        at = pl.ds(which * size, size)
        spec_ref[at, :] = times_matrix(spec_ref[at, :], mat_ref[0], mat_ref[1])

    @pl.loop(0, ROWS)
    def _(row):
        def part(which):
            at = pl.ds(pl.multiple_of((which * ROWS + row) * channels, channels), channels)
            return spec_ref[at, :INNER], spec_ref[at, INNER:]

        (hr, hi), (vr, vi), (gr, gi) = part(0), part(1), part(2)

        def put(which, re, im):
            at = pl.ds(pl.multiple_of((which * ROWS + row) * channels, channels), channels)
            prod_ref[at, :INNER] = re
            prod_ref[at, INNER:] = im

        put(0, hr * vr - hi * vi, hr * vi + hi * vr)
        put(1, hr * gr + hi * gi, hr * gi - hi * gr)
        put(2, vr * gr + vi * gi, vr * gi - vi * gr)

    for which in range(3):
        at = pl.ds(which * size, size)
        prod_ref[at, :] = times_matrix(prod_ref[at, :], mat_ref[2], mat_ref[3])

    def turned_row(which):
        def load(row):
            cos = turn_ref[2, row][None, :]
            sin = turn_ref[3, row][None, :]
            at = pl.ds((which * ROWS + row) * channels, channels)
            re, im = prod_ref[at, :INNER], prod_ref[at, INNER:]
            return re * cos - im * sin, im * cos + re * sin

        return load

    for n, entry in enumerate(outer_inverse(turned_row(0))):
        back_ref[n, 2] = (gate_ref[n] * entry).astype(back_ref.dtype)
        gate_ref[n] = cot_ref[n].astype(jnp.float32) * entry
    for n, entry in enumerate(outer_inverse(turned_row(1))):
        gval_ref[n] = entry
    for n, entry in enumerate(outer_inverse(turned_row(2))):
        fgrad_ref[:, n * INNER : (n + 1) * INNER] = entry

    for stream, ref in enumerate((gate_ref, gval_ref)):
        for n in range(HALF):
            here = ref[n]
            after = ref[n + 1] if n + 1 < HALF else None
            total = taps_ref[stream, 0] * here
            for lead in (1, 2):
                total = total + taps_ref[stream, lead] * led(here, after, lead)
            total = total.astype(jnp.bfloat16)
            back_ref[n, stream] = total


def convolved(projected, cotangent, filters, taps):
    channels, length = filters.shape
    matrices, turns = tables()
    f32 = functools.partial(pltpu.VMEM, dtype=jnp.float32)
    return pl.pallas_call(
        conv_kernel,
        out_shape=(
            jax.ShapeDtypeStruct((HALF, 3, channels, INNER), jnp.bfloat16),
            jax.ShapeDtypeStruct((channels, length), jnp.float32),
        ),
        in_specs=[pl.BlockSpec(memory_space=pltpu.VMEM)] * 6,
        out_specs=[pl.BlockSpec(memory_space=pltpu.VMEM)] * 2,
        scratch_shapes=[
            f32((HALF, channels, INNER)),
            f32((HALF, channels, INNER)),
            f32((HALF, channels, INNER)),
            f32((HALF, channels, INNER)),
            f32((3 * ROWS * channels, 2 * INNER)),
            f32((3 * ROWS * channels, 2 * INNER)),
        ],
        compiler_params=pltpu.CompilerParams(vmem_limit_bytes=32 * 1024 * 1024),
        cost_estimate=pl.CostEstimate(flops=1_300_000_000, bytes_accessed=2_000_000, transcendentals=0),
        name="long_convolutions",
    )(projected, cotangent, filters, taps, jnp.asarray(matrices), jnp.asarray(turns))


MESH = pl.DeviceIdType.MESH
CHUNK = 512


def coords():
    dp = lax.axis_index("dp")
    context = lax.axis_index("context")
    return dp // 2, dp % 2, context // 8, (context // 2) % 4, context % 2


def device(y_hi, core, z, x, y_lo):
    return (y_hi * 2 + core, z * 8 + x * 2 + y_lo)


def greet(partner):
    pl.semaphore_signal(
        pltpu.get_barrier_semaphore(), inc=1, device_id=partner, device_id_type=MESH
    )


def remote(src, dst, send_sem, recv_sem, partner):
    return pltpu.make_async_remote_copy(
        src_ref=src,
        dst_ref=dst,
        send_sem=send_sem,
        recv_sem=recv_sem,
        device_id=partner,
        device_id_type=MESH,
    )


def greet_line():
    dp = lax.axis_index("dp")
    context = lax.axis_index("context")

    @pl.loop(1, 32)
    def _(i):
        greet((dp, lax.rem(context + i, 32)))

    @pl.loop(1, 4)
    def _(i):
        greet((lax.rem(dp + i, 4), context))


def gather_kernel(
    tok_ref, cot_ref, flat_ref,
    wide_ref, proj_ref, cotg_ref, plane_ref,
    stage, loose, wide, gathered, outgoing, total,
    load_sem, store_sem, pair_send, pair_recv, half_send, half_recv, pass_send, pass_recv,
    spread_send, spread_recv, swap_sem, proj_send, proj_recv, cot_send, cot_recv,
):
    y_hi, core, z, x, y_lo = coords()
    dp = lax.axis_index("dp")
    context = lax.axis_index("context")
    rows, part = tok_ref.shape
    sibling = device(y_hi, 1 - core, z, x, y_lo)
    opposite = device(1 - y_hi, core, z, x, y_lo)
    slot = z * 4 + x
    chunks = part // CHUNK
    flat_rows = CHUNK * 8

    def quarter(j):
        return 2 * lax.rem(y_hi + j // 2, 2) + lax.rem(core + j % 2, 2)

    def chunk_of(step):
        return quarter(step // chunks) * chunks + step % chunks

    def load(step):
        at = pl.ds(pl.multiple_of(chunk_of(step) * flat_rows, flat_rows), flat_rows)
        return pltpu.make_async_copy(flat_ref.at[at], stage.at[step % 4], load_sem.at[step % 4])

    def store(step):
        at = pl.ds(pl.multiple_of(chunk_of(step) * CHUNK, CHUNK), CHUNK)
        return pltpu.make_async_copy(wide.at[at], wide_ref.at[at], store_sem.at[step])

    def separate(first, last):
        @pl.loop(first, last)
        def _(step):
            load(step).wait()
            loose[...] = stage[step % 4].astype(jnp.float32)
            at = pl.ds(pl.multiple_of(chunk_of(step) * CHUNK, CHUNK), CHUNK)
            for stream in range(2):
                for tile in range(4):
                    column = stream * 512 + tile * INNER
                    wide[at, column : column + INNER] = loose[
                        pl.ds(2 * tile + stream, CHUNK, stride=8), :
                    ].astype(jnp.bfloat16)
            store(step).start()

            @pl.when(step + 4 < 4 * chunks)
            def _():
                load(step + 4).start()

    def multiply(j, first, last):
        for piece in range(first, last):
            at = pl.ds(pl.multiple_of((quarter(j) * chunks + piece) * CHUNK, CHUNK), CHUNK)
            total[...] += jnp.dot(
                gathered[quarter(j), :, piece * CHUNK : (piece + 1) * CHUNK],
                wide[at, :],
                preferred_element_type=jnp.float32,
            )

    for step in range(4):
        load(step).start()
    greet_line()

    @pl.loop(1, 16)
    def _(i):
        other = lax.rem(slot + i, 16)
        greet(device(y_hi, 1 - core, other // 4, other % 4, y_lo))

    pl.semaphore_wait(pltpu.get_barrier_semaphore(), 34 + 15)

    half = part // 2
    halves = [
        remote(
            tok_ref.at[:, i * half : (i + 1) * half],
            gathered.at[dp, :, i * half : (i + 1) * half],
            half_send.at[i], half_recv.at[i], opposite,
        )
        for i in range(2)
    ]
    to_sibling = remote(tok_ref, gathered.at[dp], pair_send.at[0], pair_recv.at[0], sibling)
    halves[0].start()
    to_sibling.start()
    halves[1].start()

    far = 2 * (1 - y_hi) + core

    def spread(which, i, block):
        to_x = lax.rem(x + i // 2, 4)
        to_core = i % 2
        column = pl.multiple_of(512 * to_x + 256 * to_core, 256)
        src = gathered.at[block, :, pl.ds(column, 256)]
        here = (block == z) & (to_x == x) & (to_core == core)
        there = remote(
            src, plane_ref.at[to_core, slot], spread_send.at[which * 8 + i], spread_recv.at[slot],
            device(y_hi, to_core, block, to_x, y_lo),
        )
        return here, there, src

    def spread_start(which, block):
        @pl.loop(0, 8)
        def _(i):
            here, there, src = spread(which, i, block)

            @pl.when(here)
            def _():
                pltpu.make_async_copy(src, plane_ref.at[core, slot], spread_recv.at[slot]).start()

            @pl.when(jnp.logical_not(here))
            def _():
                there.start()

    def spread_done(which, block):
        @pl.loop(0, 8)
        def _(i):
            here, there, _src = spread(which, i, block)

            @pl.when(jnp.logical_not(here))
            def _():
                there.wait_send()

    gathered[dp] = tok_ref[...]
    spread_start(0, dp)

    def cot_copy(i):
        to = lax.rem(context + i, 32)
        return remote(cot_ref.at[to], cotg_ref.at[context], cot_send.at[i], cot_recv.at[i], (dp, to))

    @pl.loop(1, 32)
    def _(i):
        cot_copy(i).start()

    cotg_ref[context] = cot_ref[context]
    total[...] = jnp.zeros_like(total)
    separate(0, 4)
    multiply(0, 0, 4)
    separate(4, 8)
    to_sibling.wait_recv()
    multiply(1, 0, 4)
    separate(8, 11)

    passed = [
        remote(
            gathered.at[far, :, i * half : (i + 1) * half],
            gathered.at[far, :, i * half : (i + 1) * half],
            pass_send.at[i], pass_recv.at[i], sibling,
        )
        for i in range(2)
    ]
    halves[0].wait_recv()
    passed[0].start()
    separate(11, 14)
    multiply(2, 0, 2)
    halves[1].wait_recv()
    passed[1].start()
    spread_start(1, far)
    separate(14, 16)
    multiply(2, 2, 4)
    passed[0].wait_recv()
    multiply(3, 0, 2)
    passed[1].wait_recv()
    multiply(3, 2, 4)
    outgoing[...] = total[...].T.astype(jnp.bfloat16).reshape(outgoing.shape)

    def proj_copy(i):
        to = lax.rem(context + i, 32)
        return remote(
            outgoing.at[:, to], proj_ref.at[context], proj_send.at[i], proj_recv.at[i], (dp, to)
        )

    @pl.loop(1, 32)
    def _(i):
        proj_copy(i).start()

    proj_ref[context] = outgoing[:, context]

    @pl.loop(0, 16)
    def _(i):
        remote(
            plane_ref.at[core, i], plane_ref.at[core, i], spread_send.at[0], spread_recv.at[i], sibling
        ).wait_recv()

    swap = remote(plane_ref.at[core], plane_ref.at[core], swap_sem.at[0], swap_sem.at[1], sibling)
    swap.start()

    @pl.loop(1, 32)
    def _(i):
        proj_copy(i).wait()
        cot_copy(i).wait()

    @pl.loop(0, 16)
    def _(step):
        store(step).wait()

    for copy in halves + [to_sibling] + passed:
        copy.wait_send()
    spread_done(0, dp)
    spread_done(1, far)
    swap.wait()


def projected_groups(tokens, cotangent, flat):
    rows, part = tokens.shape
    depth, width = 4 * part, 1024
    bf16 = functools.partial(jax.ShapeDtypeStruct, dtype=jnp.bfloat16)
    dma = lambda n: pltpu.SemaphoreType.DMA((n,))
    vmem = pl.BlockSpec(memory_space=pltpu.VMEM)
    hbm = pl.BlockSpec(memory_space=pl.ANY)
    return pl.pallas_call(
        gather_kernel,
        out_shape=(
            bf16((depth, width)),
            bf16((32, 2, 16, rows)),
            bf16((32, 16, rows)),
            bf16((2, 16, rows, 256)),
        ),
        in_specs=[vmem, vmem, hbm],
        out_specs=[hbm, vmem, vmem, vmem],
        scratch_shapes=[
            pltpu.VMEM((4, CHUNK * 8, INNER), jnp.bfloat16),
            pltpu.VMEM((CHUNK * 8, INNER), jnp.float32),
            pltpu.VMEM((depth, width), jnp.bfloat16),
            pltpu.VMEM((4, rows, part), jnp.bfloat16),
            pltpu.VMEM((2, 32, 16, rows), jnp.bfloat16),
            pltpu.VMEM((rows, width), jnp.float32),
            dma(4), dma(16), dma(1), dma(1), dma(2), dma(2), dma(2), dma(2),
            dma(16), dma(16), dma(2), dma(32), dma(32), dma(32), dma(32),
        ],
        compiler_params=pltpu.CompilerParams(
            collective_id=0, has_side_effects=True, vmem_limit_bytes=50 * 1024 * 1024
        ),
        cost_estimate=pl.CostEstimate(
            flops=2_200_000_000, bytes_accessed=36_000_000, transcendentals=0
        ),
        name="gather_and_project",
    )(tokens, cotangent, flat)


def gradient_kernel(
    back_ref, plane_ref, wide_ref,
    gated_ref, tgrad_ref, wgrad_ref,
    wide, blocks, sums, leaving, arriving, far_out, far_in, own, swap_out, swap_in,
    load_sem, proj_send, proj_recv, gated_send, gated_recv, sib_send, sib_recv, far_sem,
    ring_send, ring_recv, swap_send, swap_recv,
):
    y_hi, core, z, x, y_lo = coords()
    dp = lax.axis_index("dp")
    context = lax.axis_index("context")
    sibling = device(y_hi, 1 - core, z, x, y_lo)
    opposite = device(1 - y_hi, core, z, x, y_lo)
    slot = z * 4 + x
    depth = wide.shape[0]
    piece = depth // 16
    quarter_rows = depth // 4

    def load(i):
        at = pl.ds(pl.multiple_of(i * piece, piece), piece)
        return pltpu.make_async_copy(wide_ref.at[at], wide.at[at], load_sem.at[i])

    @pl.loop(0, 16)
    def _(i):
        load(i).start()

    greet_line()
    pl.semaphore_wait(pltpu.get_barrier_semaphore(), 34)

    def proj_copy(i):
        to = lax.rem(context + i, 32)
        to_slot = (to // 8) * 4 + (to // 2) % 4
        return remote(
            back_ref.at[to, pl.ds(0, 2)], blocks.at[to_slot, :, context],
            proj_send.at[i], proj_recv.at[i], (dp, to),
        )

    def proj_arrival(i):
        source = lax.rem(context + 32 - i, 32)
        return remote(
            back_ref.at[source, pl.ds(0, 2)], blocks.at[slot, :, source],
            proj_send.at[i], proj_recv.at[i], (dp, source),
        )

    def gated_copy(i):
        to = lax.rem(context + i, 32)
        return remote(
            back_ref.at[to, 2], gated_ref.at[context], gated_send.at[i], gated_recv.at[i], (dp, to)
        )

    @pl.loop(1, 32)
    def _(i):
        proj_copy(i).start()

    @pl.loop(1, 32)
    def _(i):
        gated_copy(i).start()

    blocks[slot, :, context] = back_ref[context, pl.ds(0, 2)]
    gated_ref[context] = back_ref[context, 2]

    @pl.loop(1, 32)
    def _(i):
        proj_arrival(i).wait_recv()

    def place(first, along, across):
        if first == "x":
            return lax.rem(z + across + 4, 4) * 4 + lax.rem(x + along + 4, 4)
        return lax.rem(z + along + 4, 4) * 4 + lax.rem(x + across + 4, 4)

    def neighbour(first, along, across):
        at = place(first, along, across)
        return device(y_hi, core, at // 4, at % 4, y_lo)

    class Unit:
        def __init__(self, number):
            self.stream = number // 2
            self.part = number % 2
            self.first = ("x", "z")[self.part]
            self.base = 20 * number
            self.started = []

        def rows(self, at, part):
            begin, count = {None: (0, 16), 0: (0, 8), 1: (8, 8)}[part]
            return blocks.at[at, self.stream, pl.ds(16 * self.part + begin, count)]

        def copy(self, index, along, across, part, step_along, step_across):
            ref = self.rows(place(self.first, along, across), part)
            return remote(
                ref, ref, ring_send.at[self.base + index], ring_recv.at[self.base + index],
                neighbour(self.first, step_along, step_across),
            )

        def send(self, *args):
            copy = self.copy(*args)
            copy.start()
            self.started.append(copy)

        def arrived(self, index, along, across, part):
            self.copy(index, along, across, part, 1, 0).wait_recv()

        def send_line(self, which, along):
            self.send(4 + 4 * which, along, 0, None, 0, 1)
            self.send(5 + 4 * which, along, 0, None, 0, -1)

        def pass_line(self, which, along):
            self.arrived(4 + 4 * which, along, -1, None)
            self.send(6 + 4 * which, along, -1, 0, 0, 1)
            self.arrived(5 + 4 * which, along, 1, None)
            self.send(7 + 4 * which, along, 1, 1, 0, -1)

        def end_line(self, which, along):
            self.arrived(6 + 4 * which, along, -2, 0)
            self.arrived(7 + 4 * which, along, 2, 1)

        def begin(self):
            self.send(0, 0, 0, None, 1, 0)
            self.send(1, 0, 0, None, -1, 0)
            self.send_line(0, 0)

        def second(self):
            self.arrived(0, -1, 0, None)
            self.send(2, -1, 0, 0, 1, 0)
            self.send_line(1, -1)
            self.arrived(1, 1, 0, None)
            self.send(3, 1, 0, 1, -1, 0)
            self.send_line(2, 1)
            self.pass_line(0, 0)

        def third(self):
            self.arrived(2, -2, 0, 0)
            self.arrived(3, 2, 0, 1)
            self.send_line(3, 2)
            self.pass_line(1, -1)
            self.pass_line(2, 1)

        def fourth(self):
            self.pass_line(3, 2)
            self.end_line(0, 0)
            self.end_line(1, -1)
            self.end_line(2, 1)
            self.end_line(3, 2)

    units = [Unit(number) for number in range(4)]

    def accumulate(stream):
        sums[:, stream] = jnp.zeros(sums.shape[:1] + sums.shape[2:], jnp.float32)

        @pl.loop(0, 16)
        def _(at):
            block = blocks[at, stream].reshape(512, INNER)
            for half in range(2):
                sums[half, stream] += jnp.dot(
                    block, plane_ref[half, at], preferred_element_type=jnp.float32
                )

    def weight_copy(stream):
        return remote(
            swap_out.at[stream], swap_in.at[stream], swap_send.at[stream], swap_recv.at[stream],
            device(y_hi, core, z, x, 1 - y_lo),
        )

    def weight_send(stream):
        accumulate(stream)
        swap_out[stream] = sums[1 - y_lo, stream].astype(jnp.bfloat16)
        weight_copy(stream).start()

    def weight_end(stream):
        weight_copy(stream).wait_recv()
        full = sums[y_lo, stream] + swap_in[stream].astype(jnp.float32)
        wgrad_ref[:, stream * 512 : (stream + 1) * 512] = full.T.astype(jnp.bfloat16)

    def product(q, put):
        held = blocks[slot].reshape(1024, INNER)

        @pl.loop(0, quarter_rows // CHUNK)
        def _(i):
            at = pl.ds(pl.multiple_of(q * quarter_rows + i * CHUNK, CHUNK), CHUNK)
            put(
                pl.ds(pl.multiple_of(i * CHUNK, CHUNK), CHUNK),
                jnp.dot(wide[at, :], held, preferred_element_type=jnp.float32),
            )

    def to_sibling(which):
        return remote(
            leaving.at[which], arriving.at[which], sib_send.at[which], sib_recv.at[which], sibling
        )

    def for_sibling(which, y):
        def put(at, value):
            leaving[which, at, :] = value.astype(jnp.bfloat16)

        product(2 * y + 1 - core, put)
        to_sibling(which).start()

    def keep(y):
        def put(at, value):
            own[at, :] = value

        product(2 * y + core, put)

    far_copy = remote(far_out, far_in, far_sem.at[0], far_sem.at[1], opposite)

    units[0].begin()
    units[1].begin()

    @pl.loop(0, 16)
    def _(i):
        load(i).wait()

    for_sibling(0, 1 - y_hi)
    units[0].second()
    units[1].second()
    units[2].begin()
    units[3].begin()
    keep(1 - y_hi)
    to_sibling(0).wait_recv()
    far_out[...] = (own[...] + arriving[0].astype(jnp.float32)).astype(jnp.bfloat16)
    far_copy.start()
    units[0].third()
    units[1].third()
    units[2].second()
    units[3].second()
    for_sibling(1, y_hi)
    units[0].fourth()
    units[1].fourth()
    units[2].third()
    units[3].third()
    weight_send(0)
    keep(y_hi)
    to_sibling(1).wait_recv()
    own[...] += arriving[1].astype(jnp.float32)
    far_copy.wait_recv()
    for i in range(4):
        at = pl.ds(i * CHUNK, CHUNK)
        tgrad_ref[:, i * CHUNK : (i + 1) * CHUNK] = (
            (own[at, :] + far_in[at, :].astype(jnp.float32)).T.astype(jnp.bfloat16)
        )
    units[2].fourth()
    units[3].fourth()
    weight_send(1)
    weight_end(0)
    weight_end(1)

    @pl.loop(1, 32)
    def _(i):
        proj_copy(i).wait_send()
        gated_copy(i).wait()

    for unit in units:
        for copy in unit.started:
            copy.wait_send()
    far_copy.wait_send()
    for i in range(2):
        to_sibling(i).wait_send()
        weight_copy(i).wait_send()


def gradients(back, plane, wide):
    depth = wide.shape[0]
    bf16 = functools.partial(jax.ShapeDtypeStruct, dtype=jnp.bfloat16)
    dma = lambda n: pltpu.SemaphoreType.DMA((n,))
    vmem = pl.BlockSpec(memory_space=pltpu.VMEM)
    hbm = pl.BlockSpec(memory_space=pl.ANY)
    return pl.pallas_call(
        gradient_kernel,
        out_shape=(
            bf16((32, 16, INNER)),
            bf16((INNER, depth // 4)),
            bf16((256, 1024)),
        ),
        in_specs=[vmem, vmem, hbm],
        out_specs=[vmem, vmem, vmem],
        scratch_shapes=[
            pltpu.VMEM((depth, 1024), jnp.bfloat16),
            pltpu.VMEM((16, 2, 32, 16, INNER), jnp.bfloat16),
            pltpu.VMEM((2, 2, 512, 256), jnp.float32),
            pltpu.VMEM((2, depth // 4, INNER), jnp.bfloat16),
            pltpu.VMEM((2, depth // 4, INNER), jnp.bfloat16),
            pltpu.VMEM((depth // 4, INNER), jnp.bfloat16),
            pltpu.VMEM((depth // 4, INNER), jnp.bfloat16),
            pltpu.VMEM((depth // 4, INNER), jnp.float32),
            pltpu.VMEM((2, 512, 256), jnp.bfloat16),
            pltpu.VMEM((2, 512, 256), jnp.bfloat16),
            dma(16), dma(32), dma(32), dma(32), dma(32), dma(2), dma(2), dma(2),
            dma(80), dma(80), dma(2), dma(2),
        ],
        compiler_params=pltpu.CompilerParams(
            collective_id=1, has_side_effects=True, vmem_limit_bytes=50 * 1024 * 1024
        ),
        cost_estimate=pl.CostEstimate(
            flops=4_400_000_000, bytes_accessed=36_000_000, transcendentals=0
        ),
        name="gradients",
    )(back, plane, wide)


def on_device(tokens, in_weight, short_taps, filters, cotangent):
    channels, length = filters.shape
    groups = lax.axis_size("context")
    rows = tokens.shape[0]
    depth, streams, slab = in_weight.shape
    tiles = slab // INNER
    flat = (
        in_weight.reshape(depth, streams, tiles, INNER)
        .transpose(0, 2, 1, 3)
        .reshape(depth * streams * tiles, INNER)
    )
    wide, proj_group, cot_group, plane = projected_groups(
        tokens, cotangent.reshape(groups, channels, rows), flat
    )
    own = lax.dynamic_slice_in_dim(short_taps, lax.axis_index("context") * channels, channels, axis=2)
    taps = jnp.broadcast_to(own[..., None], own.shape + (INNER,))
    back, filter_grad = convolved(proj_group, cot_group, filters, taps)
    gated_out, token_grad, weight_grad = gradients(back, plane, wide)
    return (
        gated_out.reshape(slab, rows),
        token_grad,
        weight_grad.reshape(weight_grad.shape[0], streams, slab),
        filter_grad,
    )


def solution(mesh):
    placed = (
        P("context", "dp"),
        P(None, None, "dp"),
        P(None, None, "dp"),
        P(("dp", "context"), None),
        P("dp", "context"),
    )
    return jax.shard_map(
        on_device,
        mesh=mesh,
        in_specs=placed,
        out_specs=(
            P("dp", "context"),
            P("context", "dp"),
            P("context", None, "dp"),
            P(("dp", "context"), None),
        ),
        check_vma=False,
    )
```

```python
import functools
import math

import jax
import jax.numpy as jnp
import numpy as np
from jax import lax
from jax.experimental import pallas as pl
from jax.experimental.pallas import tpu as pltpu
from jax.sharding import PartitionSpec as P

OUTER = 64
INNER = 128
TOTAL = OUTER * INNER
HALF = OUTER // 2
KEPT = [0, 8, 16, 24, 32] + [k1 + 8 * k2 for k1 in (1, 2, 3) for k2 in range(8)] + [4, 12, 20, 28]
ROWS = len(KEPT)


def add(a, b):
    return b if a is None else a if b is None else a + b


def neg(a):
    return None if a is None else -a


def sub(a, b):
    return a if b is None else neg(b) if a is None else a - b


def scaled(a, factor):
    if a is None or abs(factor) < 1e-12:
        return None
    if abs(factor - 1) < 1e-12:
        return a
    if abs(factor + 1) < 1e-12:
        return -a
    return a * np.float32(factor)


def cadd(a, b):
    return (add(a[0], b[0]), add(a[1], b[1]))


def csub(a, b):
    return (sub(a[0], b[0]), sub(a[1], b[1]))


def turned(a, step, count):
    step %= count
    if (8 * step) % count == 0 and (8 * step // count) % 2 == 1:
        eighth = 8 * step // count
        root = math.sqrt(0.5)
        re, im = a
        if eighth == 1:
            pair = (sub(re, im), add(re, im))
        elif eighth == 3:
            pair = (neg(add(re, im)), sub(re, im))
        elif eighth == 5:
            pair = (sub(im, re), neg(add(re, im)))
        else:
            pair = (add(re, im), sub(im, re))
        return (scaled(pair[0], root), scaled(pair[1], root))
    angle = 2 * math.pi * step / count
    cos, sin = math.cos(angle), math.sin(angle)
    return (
        sub(scaled(a[0], cos), scaled(a[1], sin)),
        add(scaled(a[0], sin), scaled(a[1], cos)),
    )


def dft(values, sign):
    count = len(values)
    if count == 1:
        return values
    even = dft(values[0::2], sign)
    odd = dft(values[1::2], sign)
    odd = [turned(entry, sign * index, count) for index, entry in enumerate(odd)]
    return [cadd(a, b) for a, b in zip(even, odd)] + [csub(a, b) for a, b in zip(even, odd)]


def outer_forward(load):
    parts = []
    for second in range(8):
        line = [(load(8 * first + second), None) if first < 4 else (None, None) for first in range(8)]
        parts.append(dft(line, -1)[:5])
    results = []
    for first in (0, 1, 2, 3, 4):
        line = [turned(parts[second][first], -second * first, OUTER) for second in range(8)]
        full = dft(line, -1)
        results += {0: full[:5], 4: full[:4]}.get(first, full)
    return results


def real_line(values, count):
    top = values[0][0]
    last = values[4][0]
    a = add(top, last)
    b = sub(top, last)
    (r1, i1), (r2, i2), (r3, i3) = values[1:4]
    s13, d13 = add(r1, r3), sub(r1, r3)
    si, di = add(i1, i3), sub(i1, i3)
    root = math.sqrt(0.5)
    p = scaled(sub(d13, si), root)
    q = scaled(add(d13, si), root)
    out = [
        add(add(a, r2), s13),
        add(sub(b, i2), p),
        sub(sub(a, r2), di),
        sub(add(b, i2), q),
    ]
    if count > 4:
        out += [
            sub(add(a, r2), s13),
            sub(sub(b, i2), p),
            add(sub(a, r2), di),
            add(add(b, i2), q),
        ]
    return out


def outer_inverse(load):
    zero = real_line([load(row) for row in range(5)], 8)
    lines = []
    for first in (1, 2, 3):
        line = dft([load(5 + 8 * (first - 1) + second) for second in range(8)], 1)
        lines.append([turned(line[second], second * first, OUTER) for second in range(8)])
    tail = dft([load(29 + second) if second < 4 else (None, None) for second in range(8)], 1)
    tail = [turned(tail[second], second, 16)[0] for second in range(8)]
    results = [None] * HALF
    for second in range(8):
        line = [(zero[second], None)] + [lines[first][second] for first in range(3)] + [(tail[second], None)]
        for first, entry in enumerate(real_line(line, 4)):
            results[8 * first + second] = entry
    return results


def tables():
    index = np.arange(INNER, dtype=np.float64)
    angle = 2 * np.pi / INNER * (np.outer(index, index) % INNER)
    cos, sin = np.cos(angle), np.sin(angle)
    wide = np.block([[cos, -sin], [sin, cos]])
    high = wide.astype(jnp.bfloat16)
    low = (wide - high.astype(np.float64)).astype(jnp.bfloat16)
    inverse = wide.T
    inverse_high = inverse.astype(jnp.bfloat16)
    inverse_low = (inverse - inverse_high.astype(np.float64)).astype(jnp.bfloat16)
    matrices = np.stack([high, low, inverse_high, inverse_low])
    turn = 2 * np.pi / TOTAL * np.outer(np.array(KEPT, np.float64), index)
    weight = np.array([1.0 if k in (0, HALF) else 2.0 for k in KEPT])[:, None] / TOTAL
    turns = np.stack([np.cos(turn), np.sin(turn), weight * np.cos(turn), weight * np.sin(turn)])
    return matrices, turns.astype(np.float32)


def times_matrix(wide, high, low):
    top = wide.astype(jnp.bfloat16)
    rest = (wide - top.astype(jnp.float32)).astype(jnp.bfloat16)
    dot = functools.partial(jnp.dot, preferred_element_type=jnp.float32)
    return dot(top, high) + (dot(rest, high) + dot(top, low))


def lagged(here, before, lag):
    lane = lax.broadcasted_iota(jnp.int32, here.shape, here.ndim - 1)
    rolled = pltpu.roll(here, lag, here.ndim - 1)
    if before is None:
        return jnp.where(lane < lag, 0.0, rolled)
    return jnp.where(lane < lag, pltpu.roll(before, lag, here.ndim - 1), rolled)


def led(here, after, lead):
    lane = lax.broadcasted_iota(jnp.int32, here.shape, here.ndim - 1)
    width = here.shape[-1]
    rolled = pltpu.roll(here, width - lead, here.ndim - 1)
    if after is None:
        return jnp.where(lane >= width - lead, 0.0, rolled)
    return jnp.where(lane >= width - lead, pltpu.roll(after, width - lead, here.ndim - 1), rolled)


MESH = pl.DeviceIdType.MESH
CHUNK = 512
PIECES = 4


def coords():
    dp = lax.axis_index("dp")
    context = lax.axis_index("context")
    return dp // 2, dp % 2, context // 8, (context // 2) % 4, context % 2


def device(y_hi, core, z, x, y_lo):
    return (y_hi * 2 + core, z * 8 + x * 2 + y_lo)


def greet(partner):
    pl.semaphore_signal(
        pltpu.get_barrier_semaphore(), inc=1, device_id=partner, device_id_type=MESH
    )


def remote(src, dst, send_sem, recv_sem, partner):
    return pltpu.make_async_remote_copy(
        src_ref=src,
        dst_ref=dst,
        send_sem=send_sem,
        recv_sem=recv_sem,
        device_id=partner,
        device_id_type=MESH,
    )


def greet_line():
    dp = lax.axis_index("dp")
    context = lax.axis_index("context")

    @pl.loop(1, 32)
    def _(i):
        greet((dp, lax.rem(context + i, 32)))

    @pl.loop(1, 4)
    def _(i):
        greet((lax.rem(dp + i, 4), context))


def block_kernel(
    tok_ref, cot_ref, filt_ref, taps_ref, mat_ref, turn_ref, flat_ref,
    gated_ref, tgrad_ref, wgrad_ref, fgrad_ref,
    stage, loose, wide, gathered, outgoing, total, plane, proj, cot,
    fields, spec, prod, gate_ref, back,
    blocks, sums, leaving, arriving, far_out, far_in, own, swap_out, swap_in,
    load_sem, in_sem, pair_sem, half_send, half_recv, pass_send, pass_recv,
    spread_send, spread_recv, plane_sem, proj_send, proj_recv, cot_send, cot_recv,
    back_send, back_recv, gated_send, gated_recv, sib_send, sib_recv, far_sem,
    ring_send, ring_recv, swap_send, swap_recv,
):
    y_hi, core, z, x, y_lo = coords()
    dp = lax.axis_index("dp")
    context = lax.axis_index("context")
    rows, part = tok_ref.shape
    channels = filt_ref.shape[0]
    sibling = device(y_hi, 1 - core, z, x, y_lo)
    opposite = device(1 - y_hi, core, z, x, y_lo)
    slot = z * 4 + x
    lanes = pl.ds(pl.multiple_of(slot * INNER, INNER), INNER)
    chunks = part // CHUNK
    flat_rows = CHUNK * 8

    def quarter(j):
        return 2 * lax.rem(y_hi + j // 2, 2) + lax.rem(core + j % 2, 2)

    def chunk_of(step):
        return quarter(step // chunks) * chunks + step % chunks

    def load(step):
        at = pl.ds(pl.multiple_of(chunk_of(step) * flat_rows, flat_rows), flat_rows)
        return pltpu.make_async_copy(flat_ref.at[at], stage.at[step % 4], load_sem.at[step % 4])

    def separate(first, last):
        @pl.loop(first, last)
        def _(step):
            load(step).wait()
            loose[...] = stage[step % 4].astype(jnp.float32)
            at = pl.ds(pl.multiple_of(chunk_of(step) * CHUNK, CHUNK), CHUNK)
            for stream in range(2):
                for tile in range(4):
                    column = stream * 512 + tile * INNER
                    wide[at, column : column + INNER] = loose[
                        pl.ds(2 * tile + stream, CHUNK, stride=8), :
                    ].astype(jnp.bfloat16)

            @pl.when(step + 4 < 4 * chunks)
            def _():
                load(step + 4).start()

    def multiply(j, first, last):
        for piece in range(first, last):
            at = pl.ds(pl.multiple_of((quarter(j) * chunks + piece) * CHUNK, CHUNK), CHUNK)
            total[...] += jnp.dot(
                gathered[quarter(j), :, piece * CHUNK : (piece + 1) * CHUNK],
                wide[at, :],
                preferred_element_type=jnp.float32,
            )

    own_tokens = pltpu.make_async_copy(tok_ref, gathered.at[dp], in_sem.at[0])
    own_cot = pltpu.make_async_copy(cot_ref.at[context], cot.at[context], in_sem.at[1])
    own_tokens.start()
    own_cot.start()
    for step in range(4):
        load(step).start()
    greet_line()

    @pl.loop(1, 16)
    def _(i):
        other = lax.rem(slot + i, 16)
        greet(device(y_hi, 1 - core, other // 4, other % 4, y_lo))

    pl.semaphore_wait(pltpu.get_barrier_semaphore(), 34 + 15)

    width = part // PIECES
    pieces = [
        remote(
            tok_ref.at[:, i * width : (i + 1) * width],
            gathered.at[dp, :, i * width : (i + 1) * width],
            half_send.at[i], half_recv.at[i], opposite,
        )
        for i in range(PIECES)
    ]
    token_pair = remote(tok_ref, gathered.at[dp], pair_sem.at[0], pair_sem.at[1], sibling)
    pieces[0].start()
    token_pair.start()
    for copy in pieces[1:]:
        copy.start()
    own_tokens.wait()
    far = 2 * (1 - y_hi) + core
    passed = [
        remote(
            gathered.at[far, :, i * width : (i + 1) * width],
            gathered.at[far, :, i * width : (i + 1) * width],
            pass_send.at[i], pass_recv.at[i], sibling,
        )
        for i in range(PIECES)
    ]

    def spread(which, i, block):
        to_x = i // 2
        to_core = i % 2
        column = pl.multiple_of(512 * to_x + 256 * to_core, 256)
        src = gathered.at[block, :, pl.ds(column, 256)]
        here = (block == z) & (to_x == x) & (to_core == core)
        there = remote(
            src, plane.at[to_core, slot], spread_send.at[which * 8 + i], spread_recv.at[slot],
            device(y_hi, to_core, block, to_x, y_lo),
        )
        return here, there, src

    def spread_start(which, block, first, last):
        @pl.loop(first, last)
        def _(i):
            here, there, src = spread(which, i, block)

            @pl.when(here)
            def _():
                pltpu.make_async_copy(src, plane.at[core, slot], spread_recv.at[slot]).start()

            @pl.when(jnp.logical_not(here))
            def _():
                there.start()

    def spread_done(which, block):
        @pl.loop(0, 8)
        def _(i):
            here, there, _src = spread(which, i, block)

            @pl.when(jnp.logical_not(here))
            def _():
                there.wait_send()

    plane_copy = remote(plane.at[core], plane.at[core], plane_sem.at[0], plane_sem.at[1], sibling)

    spread_start(0, dp, 0, 8)

    def cot_copy(i):
        to = lax.rem(context + i, 32)
        return remote(cot_ref.at[to], cot.at[context], cot_send.at[i], cot_recv.at[i], (dp, to))

    @pl.loop(1, 32)
    def _(i):
        cot_copy(i).start()

    total[...] = jnp.zeros_like(total)
    separate(0, 4)
    multiply(0, 0, 4)
    separate(4, 7)
    token_pair.wait_recv()
    for n in range(HALF):
        fields[0, n] = filt_ref[:, n * INNER : (n + 1) * INNER]
    for i in range(PIECES):
        separate(7 + (9 * i) // PIECES, 7 + (9 * (i + 1)) // PIECES)
        if i == PIECES - 1:
            multiply(1, 0, 4)
            multiply(2, 0, 3)
        pieces[i].wait_recv()
        passed[i].start()
        if i % 2 == 1 and PIECES == 4:
            spread_start(1, far, 2 * i - 2, 2 * i + 2)
    multiply(2, 3, 4)
    for i in range(PIECES):
        passed[i].wait_recv()
        multiply(3, i, i + 1)
    outgoing[...] = total[...].T.astype(jnp.bfloat16).reshape(outgoing.shape)

    def proj_copy(i):
        to = lax.rem(context + i, 32)
        return remote(outgoing.at[:, to], proj.at[context], proj_send.at[i], proj_recv.at[i], (dp, to))

    @pl.loop(1, 32)
    def _(i):
        proj_copy(i).start()

    proj[context] = outgoing[:, context]

    @pl.loop(1, 32)
    def _(i):
        cot_copy(i).wait()

    own_cot.wait()

    @pl.loop(1, 32)
    def _(i):
        proj_copy(i).wait_recv()

    def short(stream, n):
        here = proj[n, stream].astype(jnp.float32)
        before = proj[n - 1, stream].astype(jnp.float32) if n else None
        result = taps_ref[stream, 0] * here
        for lag in (1, 2):
            result = result + taps_ref[stream, lag] * lagged(here, before, lag)
        return result

    for n in range(HALF):
        gate = short(0, n)
        gate_ref[n] = gate
        fields[2, n] = cot[n].astype(jnp.float32) * gate
        fields[1, n] = short(1, n)

    size = ROWS * channels

    @pl.loop(0, 3)
    def _(which):
        for row, (re, im) in enumerate(outer_forward(lambda n: fields[which, n])):
            cos = turn_ref[0, row][None, :]
            sin = turn_ref[1, row][None, :]
            at = pl.ds(row * channels, channels)
            if im is None:
                spec[which, at, :INNER] = re * cos
                spec[which, at, INNER:] = -(re * sin)
            else:
                spec[which, at, :INNER] = re * cos + im * sin
                spec[which, at, INNER:] = im * cos - re * sin
        spec[which] = times_matrix(spec[which], mat_ref[0], mat_ref[1])

    @pl.loop(0, ROWS)
    def _(row):
        at = pl.ds(pl.multiple_of(row * channels, channels), channels)
        (hr, hi), (vr, vi), (gr, gi) = [
            (spec[which, at, :INNER], spec[which, at, INNER:]) for which in range(3)
        ]

        def put(which, re, im):
            prod[which, at, :INNER] = re
            prod[which, at, INNER:] = im

        put(0, hr * vr - hi * vi, hr * vi + hi * vr)
        put(1, hr * gr + hi * gi, hr * gi - hi * gr)
        put(2, vr * gr + vi * gi, vr * gi - vi * gr)

    @pl.loop(0, 3)
    def _(which):
        prod[which] = times_matrix(prod[which], mat_ref[2], mat_ref[3])

        def turned_row(row):
            cos = turn_ref[2, row][None, :]
            sin = turn_ref[3, row][None, :]
            at = pl.ds(row * channels, channels)
            re, im = prod[which, at, :INNER], prod[which, at, INNER:]
            return re * cos - im * sin, im * cos + re * sin

        for n, entry in enumerate(outer_inverse(turned_row)):
            fields[which, n] = entry

    for n in range(HALF):
        entry = fields[0, n]
        back[n, 2] = (gate_ref[n] * entry).astype(back.dtype)
        gate_ref[n] = cot[n].astype(jnp.float32) * entry

    for stream, load_row in enumerate((lambda n: gate_ref[n], lambda n: fields[1, n])):
        for n in range(HALF):
            here = load_row(n)
            after = load_row(n + 1) if n + 1 < HALF else None
            result = taps_ref[stream, 0] * here
            for lead in (1, 2):
                result = result + taps_ref[stream, lead] * led(here, after, lead)
            back[n, stream] = result.astype(jnp.bfloat16)

    def group_rows(group):
        return pl.ds(pl.multiple_of(group * channels, channels), channels)

    def back_copy(i):
        to = lax.rem(context + i, 32)
        to_slot = (to // 8) * 4 + (to // 2) % 4
        to_lanes = pl.ds(pl.multiple_of(to_slot * INNER, INNER), INNER)
        return remote(
            back.at[to, pl.ds(0, 2)], blocks.at[:, group_rows(context), to_lanes],
            back_send.at[i], back_recv.at[i], (dp, to),
        )

    def back_arrival(i):
        source = lax.rem(context + 32 - i, 32)
        return remote(
            back.at[source, pl.ds(0, 2)], blocks.at[:, group_rows(source), lanes],
            back_send.at[i], back_recv.at[i], (dp, source),
        )

    def gated_copy(i):
        to = lax.rem(context + i, 32)
        return remote(
            back.at[to, 2], gated_ref.at[context], gated_send.at[i], gated_recv.at[i], (dp, to)
        )

    @pl.loop(1, 32)
    def _(i):
        back_copy(i).start()

    blocks[:, group_rows(context), lanes] = back[context, pl.ds(0, 2)]

    @pl.loop(1, 32)
    def _(i):
        gated_copy(i).start()

    gated_ref[context] = back[context, 2]
    for n in range(HALF):
        fgrad_ref[:, n * INNER : (n + 1) * INNER] = fields[2, n]

    @pl.loop(0, 16)
    def _(i):
        remote(
            plane.at[core, i], plane.at[core, i], spread_send.at[0], spread_recv.at[i], sibling
        ).wait_recv()

    plane_copy.start()

    @pl.loop(1, 32)
    def _(i):
        back_arrival(i).wait_recv()

    def place(first, along, across):
        if first == "x":
            return lax.rem(z + across + 4, 4) * 4 + lax.rem(x + along + 4, 4)
        return lax.rem(z + along + 4, 4) * 4 + lax.rem(x + across + 4, 4)

    def neighbour(first, along, across):
        at = place(first, along, across)
        return device(y_hi, core, at // 4, at % 4, y_lo)

    class Unit:
        def __init__(self, number):
            self.stream = number // 2
            self.part = number % 2
            self.first = ("x", "z")[self.part]
            self.base = 20 * number
            self.started = []

        def rows(self, at, part):
            begin, count = {None: (0, 256), 0: (0, 128), 1: (128, 128)}[part]
            return blocks.at[
                self.stream,
                pl.ds(256 * self.part + begin, count),
                pl.ds(pl.multiple_of(at * INNER, INNER), INNER),
            ]

        def copy(self, index, along, across, part, step_along, step_across):
            ref = self.rows(place(self.first, along, across), part)
            return remote(
                ref, ref, ring_send.at[self.base + index], ring_recv.at[self.base + index],
                neighbour(self.first, step_along, step_across),
            )

        def send(self, *args):
            copy = self.copy(*args)
            copy.start()
            self.started.append(copy)

        def arrived(self, index, along, across, part):
            self.copy(index, along, across, part, 1, 0).wait_recv()

        def send_line(self, which, along):
            self.send(4 + 4 * which, along, 0, None, 0, 1)
            self.send(5 + 4 * which, along, 0, None, 0, -1)

        def pass_line(self, which, along):
            self.arrived(4 + 4 * which, along, -1, None)
            self.send(6 + 4 * which, along, -1, 0, 0, 1)
            self.arrived(5 + 4 * which, along, 1, None)
            self.send(7 + 4 * which, along, 1, 1, 0, -1)

        def end_line(self, which, along):
            self.arrived(6 + 4 * which, along, -2, 0)
            self.arrived(7 + 4 * which, along, 2, 1)

        def begin(self):
            self.send(0, 0, 0, None, 1, 0)
            self.send(1, 0, 0, None, -1, 0)
            self.send_line(0, 0)

        def second(self):
            self.arrived(0, -1, 0, None)
            self.send(2, -1, 0, 0, 1, 0)
            self.send_line(1, -1)
            self.arrived(1, 1, 0, None)
            self.send(3, 1, 0, 1, -1, 0)
            self.send_line(2, 1)
            self.pass_line(0, 0)

        def third(self):
            self.arrived(2, -2, 0, 0)
            self.arrived(3, 2, 0, 1)
            self.send_line(3, 2)
            self.pass_line(1, -1)
            self.pass_line(2, 1)

        def fourth(self):
            self.pass_line(3, 2)

        def end(self):
            self.end_line(0, 0)
            self.end_line(1, -1)
            self.end_line(2, 1)
            self.end_line(3, 2)

    units = [Unit(number) for number in range(4)]

    def weight_copy(stream):
        return remote(
            swap_out.at[stream], swap_in.at[stream], swap_send.at[stream], swap_recv.at[stream],
            device(y_hi, core, z, x, 1 - y_lo),
        )

    def weight_sum(stream, half):
        return jnp.dot(
            blocks[stream], plane[half].reshape(16 * INNER, 256), preferred_element_type=jnp.float32
        )

    def weight_send(stream):
        swap_out[stream] = weight_sum(stream, 1 - y_lo).astype(jnp.bfloat16)
        weight_copy(stream).start()
        sums[stream] = weight_sum(stream, y_lo)

    def weight_end(stream):
        weight_copy(stream).wait_recv()
        full = sums[stream] + swap_in[stream].astype(jnp.float32)
        wgrad_ref[:, stream * 512 : (stream + 1) * 512] = full.T.astype(jnp.bfloat16)

    def product(q, put, first, last):
        held = blocks[:, :, lanes].reshape(1024, INNER)
        for i in range(first, last):
            at = pl.ds(pl.multiple_of(q * part + i * CHUNK, CHUNK), CHUNK)
            put(
                pl.ds(i * CHUNK, CHUNK),
                jnp.dot(wide[at, :], held, preferred_element_type=jnp.float32),
            )

    def to_sibling(which):
        return remote(
            leaving.at[which], arriving.at[which], sib_send.at[which], sib_recv.at[which], sibling
        )

    def for_sibling(which, y, first, last):
        def put(at, value):
            leaving[which, at, :] = value.astype(jnp.bfloat16)

        product(2 * y + 1 - core, put, first, last)
        if last == chunks:
            to_sibling(which).start()

    def keep(y, first, last):
        def put(at, value):
            own[at, :] = value

        product(2 * y + core, put, first, last)

    far_copy = remote(far_out, far_in, far_sem.at[0], far_sem.at[1], opposite)

    units[0].begin()
    units[1].begin()
    for_sibling(0, 1 - y_hi, 0, 4)
    units[0].second()
    units[1].second()
    units[2].begin()
    units[3].begin()
    keep(1 - y_hi, 0, 4)
    units[0].third()
    units[1].third()
    to_sibling(0).wait_recv()
    far_out[...] = (own[...] + arriving[0].astype(jnp.float32)).astype(jnp.bfloat16)
    far_copy.start()
    units[2].second()
    units[3].second()
    units[0].fourth()
    units[1].fourth()
    for_sibling(1, y_hi, 0, 4)
    units[2].third()
    units[3].third()
    units[0].end()
    units[1].end()
    plane_copy.wait_recv()
    weight_send(0)
    units[2].fourth()
    units[3].fourth()
    keep(y_hi, 0, 4)
    to_sibling(1).wait_recv()
    own[...] += arriving[1].astype(jnp.float32)
    units[2].end()
    units[3].end()
    weight_send(1)
    weight_end(0)
    far_copy.wait_recv()
    for i in range(chunks):
        at = pl.ds(i * CHUNK, CHUNK)
        tgrad_ref[:, i * CHUNK : (i + 1) * CHUNK] = (
            (own[at, :] + far_in[at, :].astype(jnp.float32)).T.astype(jnp.bfloat16)
        )

    @pl.loop(1, 32)
    def _(i):
        proj_copy(i).wait_send()
        back_copy(i).wait_send()
        gated_copy(i).wait()

    for copy in pieces + passed + [token_pair, plane_copy, far_copy]:
        copy.wait_send()
    spread_done(0, dp)
    spread_done(1, far)
    for unit in units:
        for copy in unit.started:
            copy.wait_send()
    for i in range(2):
        to_sibling(i).wait_send()
        weight_copy(i).wait_send()
    weight_end(1)


def on_device(tokens, in_weight, short_taps, filters, cotangent):
    channels, length = filters.shape
    groups = lax.axis_size("context")
    rows, part = tokens.shape
    depth, streams, slab = in_weight.shape
    tiles = slab // INNER
    flat = (
        in_weight.reshape(depth, streams, tiles, INNER)
        .transpose(0, 2, 1, 3)
        .reshape(depth * streams * tiles, INNER)
    )
    taps = lax.dynamic_slice_in_dim(short_taps, lax.axis_index("context") * channels, channels, axis=2)
    taps = jnp.broadcast_to(taps[..., None], taps.shape + (INNER,))
    matrices, turns = tables()
    vmem = pl.BlockSpec(memory_space=pltpu.VMEM)
    hbm = pl.BlockSpec(memory_space=pl.ANY)

    def bf16(*shape):
        return pltpu.VMEM(shape, jnp.bfloat16)

    def f32(*shape):
        return pltpu.VMEM(shape, jnp.float32)

    def dma(*counts):
        return [pltpu.SemaphoreType.DMA((count,)) for count in counts]

    size = ROWS * channels
    gated_out, token_grad, weight_grad, filter_grad = pl.pallas_call(
        block_kernel,
        out_shape=(
            jax.ShapeDtypeStruct((groups, channels, rows), jnp.bfloat16),
            jax.ShapeDtypeStruct((rows, part), jnp.bfloat16),
            jax.ShapeDtypeStruct((256, streams * slab), jnp.bfloat16),
            jax.ShapeDtypeStruct((channels, length), jnp.float32),
        ),
        in_specs=[hbm, hbm, vmem, vmem, vmem, vmem, hbm],
        out_specs=[vmem] * 4,
        scratch_shapes=[
            bf16(4, CHUNK * 8, INNER),
            f32(CHUNK * 8, INNER),
            bf16(depth, streams * slab),
            bf16(4, rows, part),
            bf16(streams, groups, channels, rows),
            f32(rows, streams * slab),
            bf16(2, 16, rows, 256),
            bf16(groups, streams, channels, rows),
            bf16(groups, channels, rows),
            f32(3, HALF, channels, INNER),
            f32(3, size, 2 * INNER),
            f32(3, size, 2 * INNER),
            f32(HALF, channels, INNER),
            bf16(groups, 3, channels, rows),
            bf16(streams, slab, 16 * rows),
            f32(streams, slab, 256),
            bf16(2, part, rows),
            bf16(2, part, rows),
            bf16(part, rows),
            bf16(part, rows),
            f32(part, rows),
            bf16(streams, slab, 256),
            bf16(streams, slab, 256),
            *dma(4, 2, 2, PIECES, PIECES, PIECES, PIECES, 16, 16, 2, 32, 32, 32, 32),
            *dma(32, 32, 32, 32, 2, 2, 2, 80, 80, 2, 2),
        ],
        compiler_params=pltpu.CompilerParams(
            collective_id=0, has_side_effects=True, vmem_limit_bytes=56 * 1024 * 1024
        ),
        cost_estimate=pl.CostEstimate(
            flops=8_000_000_000, bytes_accessed=24_000_000, transcendentals=0
        ),
        name="block_forward_backward",
    )(
        tokens, cotangent.reshape(groups, channels, rows), filters, taps,
        jnp.asarray(matrices), jnp.asarray(turns), flat,
    )
    return (
        gated_out.reshape(slab, rows),
        token_grad,
        weight_grad.reshape(weight_grad.shape[0], streams, slab),
        filter_grad,
    )


def solution(mesh):
    placed = (
        P("context", "dp"),
        P(None, None, "dp"),
        P(None, None, "dp"),
        P(("dp", "context"), None),
        P("dp", "context"),
    )
    return jax.shard_map(
        on_device,
        mesh=mesh,
        in_specs=placed,
        out_specs=(
            P("dp", "context"),
            P("context", "dp"),
            P("context", None, "dp"),
            P(("dp", "context"), None),
        ),
        check_vma=False,
    )
```

```python
import functools
import math

import jax
import jax.numpy as jnp
import numpy as np
from jax import lax
from jax.experimental import pallas as pl
from jax.experimental.pallas import tpu as pltpu
from jax.sharding import PartitionSpec as P

OUTER = 64
INNER = 128
TOTAL = OUTER * INNER
HALF = OUTER // 2
KEPT = [0, 8, 16, 24, 32] + [k1 + 8 * k2 for k1 in (1, 2, 3) for k2 in range(8)] + [4, 12, 20, 28]
ROWS = len(KEPT)


def add(a, b):
    return b if a is None else a if b is None else a + b


def neg(a):
    return None if a is None else -a


def sub(a, b):
    return a if b is None else neg(b) if a is None else a - b


def scaled(a, factor):
    if a is None or abs(factor) < 1e-12:
        return None
    if abs(factor - 1) < 1e-12:
        return a
    if abs(factor + 1) < 1e-12:
        return -a
    return a * np.float32(factor)


def cadd(a, b):
    return (add(a[0], b[0]), add(a[1], b[1]))


def csub(a, b):
    return (sub(a[0], b[0]), sub(a[1], b[1]))


def turned(a, step, count):
    step %= count
    if (8 * step) % count == 0 and (8 * step // count) % 2 == 1:
        eighth = 8 * step // count
        root = math.sqrt(0.5)
        re, im = a
        if eighth == 1:
            pair = (sub(re, im), add(re, im))
        elif eighth == 3:
            pair = (neg(add(re, im)), sub(re, im))
        elif eighth == 5:
            pair = (sub(im, re), neg(add(re, im)))
        else:
            pair = (add(re, im), sub(im, re))
        return (scaled(pair[0], root), scaled(pair[1], root))
    angle = 2 * math.pi * step / count
    cos, sin = math.cos(angle), math.sin(angle)
    return (
        sub(scaled(a[0], cos), scaled(a[1], sin)),
        add(scaled(a[0], sin), scaled(a[1], cos)),
    )


def dft(values, sign):
    count = len(values)
    if count == 1:
        return values
    even = dft(values[0::2], sign)
    odd = dft(values[1::2], sign)
    odd = [turned(entry, sign * index, count) for index, entry in enumerate(odd)]
    return [cadd(a, b) for a, b in zip(even, odd)] + [csub(a, b) for a, b in zip(even, odd)]


def outer_forward(load):
    parts = []
    for second in range(8):
        line = [(load(8 * first + second), None) if first < 4 else (None, None) for first in range(8)]
        parts.append(dft(line, -1)[:5])
    results = []
    for first in (0, 1, 2, 3, 4):
        line = [turned(parts[second][first], -second * first, OUTER) for second in range(8)]
        full = dft(line, -1)
        results += {0: full[:5], 4: full[:4]}.get(first, full)
    return results


def real_line(values, count):
    top = values[0][0]
    last = values[4][0]
    a = add(top, last)
    b = sub(top, last)
    (r1, i1), (r2, i2), (r3, i3) = values[1:4]
    s13, d13 = add(r1, r3), sub(r1, r3)
    si, di = add(i1, i3), sub(i1, i3)
    root = math.sqrt(0.5)
    p = scaled(sub(d13, si), root)
    q = scaled(add(d13, si), root)
    out = [
        add(add(a, r2), s13),
        add(sub(b, i2), p),
        sub(sub(a, r2), di),
        sub(add(b, i2), q),
    ]
    if count > 4:
        out += [
            sub(add(a, r2), s13),
            sub(sub(b, i2), p),
            add(sub(a, r2), di),
            add(add(b, i2), q),
        ]
    return out


def outer_inverse(load):
    zero = real_line([load(row) for row in range(5)], 8)
    lines = []
    for first in (1, 2, 3):
        line = dft([load(5 + 8 * (first - 1) + second) for second in range(8)], 1)
        lines.append([turned(line[second], second * first, OUTER) for second in range(8)])
    tail = dft([load(29 + second) if second < 4 else (None, None) for second in range(8)], 1)
    tail = [turned(tail[second], second, 16)[0] for second in range(8)]
    results = [None] * HALF
    for second in range(8):
        line = [(zero[second], None)] + [lines[first][second] for first in range(3)] + [(tail[second], None)]
        for first, entry in enumerate(real_line(line, 4)):
            results[8 * first + second] = entry
    return results


def tables():
    index = np.arange(INNER, dtype=np.float64)
    angle = 2 * np.pi / INNER * (np.outer(index, index) % INNER)
    cos, sin = np.cos(angle), np.sin(angle)
    wide = np.block([[cos, -sin], [sin, cos]])
    high = wide.astype(jnp.bfloat16)
    low = (wide - high.astype(np.float64)).astype(jnp.bfloat16)
    inverse = wide.T
    inverse_high = inverse.astype(jnp.bfloat16)
    inverse_low = (inverse - inverse_high.astype(np.float64)).astype(jnp.bfloat16)
    matrices = np.stack([high, low, inverse_high, inverse_low])
    turn = 2 * np.pi / TOTAL * np.outer(np.array(KEPT, np.float64), index)
    weight = np.array([1.0 if k in (0, HALF) else 2.0 for k in KEPT])[:, None] / TOTAL
    turns = np.stack([np.cos(turn), np.sin(turn), weight * np.cos(turn), weight * np.sin(turn)])
    return matrices, turns.astype(np.float32)


def times_matrix(wide, high, low):
    top = wide.astype(jnp.bfloat16)
    rest = (wide - top.astype(jnp.float32)).astype(jnp.bfloat16)
    dot = functools.partial(jnp.dot, preferred_element_type=jnp.float32)
    return dot(top, high) + (dot(rest, high) + dot(top, low))


def lagged(here, before, lag):
    lane = lax.broadcasted_iota(jnp.int32, here.shape, here.ndim - 1)
    rolled = pltpu.roll(here, lag, here.ndim - 1)
    if before is None:
        return jnp.where(lane < lag, 0.0, rolled)
    return jnp.where(lane < lag, pltpu.roll(before, lag, here.ndim - 1), rolled)


def led(here, after, lead):
    lane = lax.broadcasted_iota(jnp.int32, here.shape, here.ndim - 1)
    width = here.shape[-1]
    rolled = pltpu.roll(here, width - lead, here.ndim - 1)
    if after is None:
        return jnp.where(lane >= width - lead, 0.0, rolled)
    return jnp.where(lane >= width - lead, pltpu.roll(after, width - lead, here.ndim - 1), rolled)


MESH = pl.DeviceIdType.MESH
CHUNK = 512
PIECES = 4


def coords():
    dp = lax.axis_index("dp")
    context = lax.axis_index("context")
    return dp // 2, dp % 2, context // 8, (context // 2) % 4, context % 2


def device(y_hi, core, z, x, y_lo):
    return (y_hi * 2 + core, z * 8 + x * 2 + y_lo)


def greet(partner):
    pl.semaphore_signal(
        pltpu.get_barrier_semaphore(), inc=1, device_id=partner, device_id_type=MESH
    )


def remote(src, dst, send_sem, recv_sem, partner):
    return pltpu.make_async_remote_copy(
        src_ref=src,
        dst_ref=dst,
        send_sem=send_sem,
        recv_sem=recv_sem,
        device_id=partner,
        device_id_type=MESH,
    )


def greet_line():
    dp = lax.axis_index("dp")
    context = lax.axis_index("context")

    @pl.loop(1, 32)
    def _(i):
        greet((dp, lax.rem(context + i, 32)))

    @pl.loop(1, 4)
    def _(i):
        greet((lax.rem(dp + i, 4), context))


def block_kernel(
    tok_ref, cot_ref, filt_hbm, taps_ref, mat_hbm, turn_hbm, flat_ref,
    gated_hbm, tgrad_hbm, wgrad_hbm, fgrad_hbm,
    filt_ref, mat_ref, turn_ref, gated_ref, tgrad_ref, wgrad_ref, wgrad_rows, fgrad_ref, out_sem,
    stage, loose, wide, gathered, outgoing, total, plane, proj, cot,
    fields, spec, prod, gate_ref, gated_group,
    ours, blocks, held, sums, leaving, arriving, far_out, far_in, own, swap_out, swap_in,
    load_sem, in_sem, pair_sem, half_send, half_recv, pass_send, pass_recv,
    spread_send, spread_recv, plane_sem, proj_send, proj_recv, cot_send, cot_recv,
    back_send, back_recv, gated_send, gated_recv, sib_send, sib_recv, far_sem,
    ring_send, ring_recv, swap_send, swap_recv,
):
    y_hi, core, z, x, y_lo = coords()
    dp = lax.axis_index("dp")
    context = lax.axis_index("context")
    rows, part = tok_ref.shape
    channels = filt_hbm.shape[0]
    size = ROWS * channels
    sibling = device(y_hi, 1 - core, z, x, y_lo)
    opposite = device(1 - y_hi, core, z, x, y_lo)
    slot = z * 4 + x
    chunks = part // CHUNK
    flat_rows = CHUNK * 8

    def quarter(j):
        return 2 * lax.rem(y_hi + j // 2, 2) + lax.rem(core + j % 2, 2)

    def chunk_of(step):
        return quarter(step // chunks) * chunks + step % chunks

    def load(step):
        at = pl.ds(pl.multiple_of(chunk_of(step) * flat_rows, flat_rows), flat_rows)
        return pltpu.make_async_copy(flat_ref.at[at], stage.at[step % 4], load_sem.at[step % 4])

    def cot_copy(i):
        to = lax.rem(context + i, 32)
        return remote(cot_ref.at[to], cot.at[context], cot_send.at[i], cot_recv.at[i], (dp, to))

    def separate(first, last, sends=False):
        @pl.loop(first, last)
        def _(step):
            load(step).wait()
            loose[...] = stage[step % 4].astype(jnp.float32)
            at = pl.ds(pl.multiple_of(chunk_of(step) * CHUNK, CHUNK), CHUNK)
            for stream in range(2):
                for tile in range(4):
                    column = stream * 512 + tile * INNER
                    wide[at, column : column + INNER] = loose[
                        pl.ds(2 * tile + stream, CHUNK, stride=8), :
                    ].astype(jnp.bfloat16)

            @pl.when(step + 4 < 4 * chunks)
            def _():
                load(step + 4).start()

            for j in range(4 if sends else 0):
                to = 1 + (step - first) * 4 + j

                @pl.when(to < 32)
                def _():
                    cot_copy(to).start()

    def multiply(j, first, last):
        for piece in range(first, last):
            at = pl.ds(pl.multiple_of((quarter(j) * chunks + piece) * CHUNK, CHUNK), CHUNK)
            total[...] += jnp.dot(
                gathered[quarter(j), :, piece * CHUNK : (piece + 1) * CHUNK],
                wide[at, :],
                preferred_element_type=jnp.float32,
            )

    own_tokens = pltpu.make_async_copy(tok_ref, gathered.at[dp], in_sem.at[0])
    own_cot = pltpu.make_async_copy(cot_ref.at[context], cot.at[context], in_sem.at[1])
    own_tables = [
        pltpu.make_async_copy(src, dst, in_sem.at[2 + i])
        for i, (src, dst) in enumerate(((filt_hbm, filt_ref), (mat_hbm, mat_ref), (turn_hbm, turn_ref)))
    ]
    for step in range(4):
        load(step).start()
    own_tokens.start()
    own_cot.start()
    for copy in own_tables:
        copy.start()
    greet_line()

    @pl.loop(1, 16)
    def _(i):
        other = lax.rem(slot + i, 16)
        greet(device(y_hi, 1 - core, other // 4, other % 4, y_lo))

    separate(0, 3)
    pl.semaphore_wait(pltpu.get_barrier_semaphore(), 34 + 15)

    width = part // PIECES
    pieces = [
        remote(
            tok_ref.at[:, i * width : (i + 1) * width],
            gathered.at[dp, :, i * width : (i + 1) * width],
            half_send.at[i], half_recv.at[i], opposite,
        )
        for i in range(PIECES)
    ]
    token_pair = remote(tok_ref, gathered.at[dp], pair_sem.at[0], pair_sem.at[1], sibling)
    pieces[0].start()
    token_pair.start()
    for copy in pieces[1:]:
        copy.start()
    own_tokens.wait()
    far = 2 * (1 - y_hi) + core
    passed = [
        remote(
            gathered.at[far, :, i * width : (i + 1) * width],
            gathered.at[far, :, i * width : (i + 1) * width],
            pass_send.at[i], pass_recv.at[i], sibling,
        )
        for i in range(PIECES)
    ]

    def spread(which, i, block):
        to_x = i // 2
        to_core = i % 2
        column = pl.multiple_of(512 * to_x + 256 * to_core, 256)
        src = gathered.at[block, :, pl.ds(column, 256)]
        here = (block == z) & (to_x == x) & (to_core == core)
        there = remote(
            src, plane.at[to_core, slot], spread_send.at[which * 8 + i], spread_recv.at[slot],
            device(y_hi, to_core, block, to_x, y_lo),
        )
        return here, there, src

    def spread_start(which, block, first, last):
        @pl.loop(first, last)
        def _(i):
            here, there, src = spread(which, i, block)

            @pl.when(here)
            def _():
                pltpu.make_async_copy(src, plane.at[core, slot], spread_recv.at[slot]).start()

            @pl.when(jnp.logical_not(here))
            def _():
                there.start()

    def spread_done(which, block):
        @pl.loop(0, 8)
        def _(i):
            here, there, _src = spread(which, i, block)

            @pl.when(jnp.logical_not(here))
            def _():
                there.wait_send()

    across = device(y_hi, core, z, x, 1 - y_lo)
    plane_pair = remote(plane.at[core], plane.at[core], plane_sem.at[0], plane_sem.at[1], sibling)

    spread_start(0, dp, 0, 8)

    total[...] = jnp.zeros_like(total)
    separate(3, 11, True)
    multiply(0, 0, 4)
    token_pair.wait_recv()
    for i in range(PIECES):
        if i < 3:
            pieces[i].wait_recv()
            passed[i].start()
            spread_start(1, far, 2 * i, 2 * i + 2)
            separate(11 + i, 12 + i)
        else:
            separate(14, 16)
            multiply(1, 0, 4)
            multiply(2, 0, 3)
            for n in range(3):
                passed[n].wait_recv()
                multiply(3, n, n + 1)
            pieces[i].wait_recv()
            passed[i].start()
            multiply(2, 3, 4)
            passed[3].wait_recv()
            multiply(3, 3, 4)
    def transform(begin, end):
        @pl.loop(begin, end)
        def _(which):
            for row, (re, im) in enumerate(outer_forward(lambda n: fields[which, n])):
                cos = turn_ref[0, row][None, :]
                sin = turn_ref[1, row][None, :]
                at = pl.ds(row * channels, channels)
                if im is None:
                    spec[which, at, :INNER] = re * cos
                    spec[which, at, INNER:] = -(re * sin)
                else:
                    spec[which, at, :INNER] = re * cos + im * sin
                    spec[which, at, INNER:] = im * cos - re * sin
            spec[which] = times_matrix(spec[which], mat_ref[0], mat_ref[1])

    outgoing[...] = total[...].T.astype(jnp.bfloat16).reshape(outgoing.shape)

    def proj_copy(i):
        to = lax.rem(context + i, 32)
        return remote(outgoing.at[:, to], proj.at[context], proj_send.at[i], proj_recv.at[i], (dp, to))

    @pl.loop(1, 32)
    def _(i):
        proj_copy(i).start()

    proj[context] = outgoing[:, context]
    spread_start(1, far, 6, 8)
    for copy in own_tables:
        copy.wait()
    for n in range(HALF):
        fields[0, n] = filt_ref[:, n * INNER : (n + 1) * INNER]

    @pl.loop(1, 32)
    def _(i):
        cot_copy(i).wait_recv()

    own_cot.wait()

    @pl.loop(1, 32)
    def _(i):
        proj_copy(i).wait_recv()

    def short(stream, n):
        here = proj[n, stream].astype(jnp.float32)
        before = proj[n - 1, stream].astype(jnp.float32) if n else None
        result = taps_ref[stream, 0] * here
        for lag in (1, 2):
            result = result + taps_ref[stream, lag] * lagged(here, before, lag)
        return result

    for n in range(HALF):
        gate = short(0, n)
        gate_ref[n] = gate
        fields[2, n] = cot[n].astype(jnp.float32) * gate
        fields[1, n] = short(1, n)

    transform(0, 3)

    @pl.loop(0, ROWS)
    def _(row):
        at = pl.ds(pl.multiple_of(row * channels, channels), channels)
        (hr, hi), (vr, vi), (gr, gi) = [
            (spec[which, at, :INNER], spec[which, at, INNER:]) for which in range(3)
        ]

        def put(which, re, im):
            prod[which, at, :INNER] = re
            prod[which, at, INNER:] = im

        put(0, hr * vr - hi * vi, hr * vi + hi * vr)
        put(1, hr * gr + hi * gi, hr * gi - hi * gr)
        put(2, vr * gr + vi * gi, vr * gi - vi * gr)

    @pl.loop(0, 3)
    def _(which):
        prod[which] = times_matrix(prod[which], mat_ref[2], mat_ref[3])

        def turned_row(row):
            cos = turn_ref[2, row][None, :]
            sin = turn_ref[3, row][None, :]
            at = pl.ds(row * channels, channels)
            re, im = prod[which, at, :INNER], prod[which, at, INNER:]
            return re * cos - im * sin, im * cos + re * sin

        for n, entry in enumerate(outer_inverse(turned_row)):
            fields[which, n] = entry

    for n in range(HALF):
        entry = fields[0, n]
        gated_group[n] = (gate_ref[n] * entry).astype(jnp.bfloat16)
        gate_ref[n] = cot[n].astype(jnp.float32) * entry

    for stream, load_row in enumerate((lambda n: gate_ref[n], lambda n: fields[1, n])):
        for n in range(HALF):
            here = load_row(n)
            after = load_row(n + 1) if n + 1 < HALF else None
            result = taps_ref[stream, 0] * here
            for lead in (1, 2):
                result = result + taps_ref[stream, lead] * led(here, after, lead)
            column = n // 2 * INNER
            ours[stream, n % 2, :, column : column + INNER] = result.astype(jnp.bfloat16)

    def group_rows(group):
        return pl.ds(pl.multiple_of(group * channels, channels), channels)

    def column_of(index):
        return pl.ds(pl.multiple_of(index // 2 * INNER, INNER), INNER)

    def back_copy(i):
        to = lax.rem(context + i, 32)
        return remote(
            ours.at[:, to % 2, :, column_of(to)], held.at[:, group_rows(context)],
            back_send.at[i], back_recv.at[i], (dp, to),
        )

    def back_arrival(i):
        source = lax.rem(context + 32 - i, 32)
        return remote(
            ours.at[:, source % 2, :, column_of(source)], held.at[:, group_rows(source)],
            back_send.at[i], back_recv.at[i], (dp, source),
        )

    ours_across = remote(
        ours.at[:, 1 - y_lo], blocks.at[:, group_rows(context)], plane_sem.at[2], plane_sem.at[3], across
    )

    def gated_copy(i):
        to = lax.rem(context + i, 32)
        return remote(
            gated_group.at[to], gated_ref.at[context], gated_send.at[i], gated_recv.at[i], (dp, to)
        )

    def leave(which):
        src, dst = (
            (gated_ref, gated_hbm), (tgrad_ref, tgrad_hbm), (wgrad_ref, wgrad_hbm), (fgrad_ref, fgrad_hbm),
        )[which]
        return pltpu.make_async_copy(src, dst, out_sem.at[which])

    @pl.loop(1, 32)
    def _(i):
        back_copy(i).start()

    ours_across.start()
    blocks[:, group_rows(context)] = ours[:, y_lo]

    def place(first, along, aside):
        if first == "x":
            return lax.rem(z + aside + 4, 4) * 4 + lax.rem(x + along + 4, 4)
        return lax.rem(z + along + 4, 4) * 4 + lax.rem(x + aside + 4, 4)

    def neighbour(first, along, aside):
        at = place(first, along, aside)
        return device(y_hi, core, at // 4, at % 4, y_lo)

    class Unit:
        def __init__(self, number):
            self.stream = number // 2
            self.from_y = (y_lo, 1 - y_lo)[number % 2]
            self.first = ("x", "z")[number % 2]
            self.base = 20 * number
            self.started = []

        def copy(self, index, along, aside, part, step_along, step_aside):
            begin, count = {None: (0, 2048), 0: (0, 1024), 1: (1024, 1024)}[part]
            ref = blocks.at[
                self.stream,
                group_rows(2 * place(self.first, along, aside) + self.from_y),
                pl.ds(begin, count),
            ]
            return remote(
                ref, ref, ring_send.at[self.base + index], ring_recv.at[self.base + index],
                neighbour(self.first, step_along, step_aside),
            )

        def send(self, *args):
            copy = self.copy(*args)
            copy.start()
            self.started.append(copy)

        def arrived(self, index, along, aside, part):
            self.copy(index, along, aside, part, 1, 0).wait_recv()

        def send_line(self, which, along):
            self.send(4 + 4 * which, along, 0, None, 0, 1)
            self.send(5 + 4 * which, along, 0, None, 0, -1)

        def pass_line(self, which, along):
            self.arrived(4 + 4 * which, along, -1, None)
            self.send(6 + 4 * which, along, -1, 0, 0, 1)
            self.arrived(5 + 4 * which, along, 1, None)
            self.send(7 + 4 * which, along, 1, 1, 0, -1)

        def begin(self):
            self.send(0, 0, 0, None, 1, 0)
            self.send(1, 0, 0, None, -1, 0)

        def relay(self):
            self.arrived(0, -1, 0, None)
            self.send(2, -1, 0, 0, 1, 0)
            self.arrived(1, 1, 0, None)
            self.send(3, 1, 0, 1, -1, 0)

        def lines(self):
            self.send_line(1, -1)
            self.send_line(2, 1)

        def last_line(self):
            self.arrived(2, -2, 0, 0)
            self.arrived(3, 2, 0, 1)
            self.send_line(3, 2)

        def end(self):
            for which, along in enumerate((0, -1, 1, 2)):
                self.arrived(6 + 4 * which, along, -2, 0)
                self.arrived(7 + 4 * which, along, 2, 1)

    units = [Unit(number) for number in range(4)]

    def weight_copy(stream):
        return remote(
            swap_out.at[stream], swap_in.at[stream], swap_send.at[stream], swap_recv.at[stream], across
        )

    def weight_sum(stream, half):
        return jnp.dot(
            blocks[stream], plane[half].reshape(16 * INNER, 256), preferred_element_type=jnp.float32
        )

    def weight_send(stream):
        swap_out[stream] = weight_sum(stream, 1 - y_lo).astype(jnp.bfloat16)
        weight_copy(stream).start()
        sums[stream] = weight_sum(stream, y_lo)

    def weight_end(stream):
        weight_copy(stream).wait_recv()
        turned_sum = (sums[stream] + swap_in[stream].astype(jnp.float32)).T
        for tile in range(4):
            wgrad_rows[pl.ds(2 * tile + stream, 256, stride=8), :] = turned_sum[
                :, tile * INNER : (tile + 1) * INNER
            ]

    def product(q, put, first, last):
        shard = held[...].reshape(1024, INNER)
        for i in range(first, last):
            at = pl.ds(pl.multiple_of(q * part + i * CHUNK, CHUNK), CHUNK)
            put(
                pl.ds(i * CHUNK, CHUNK),
                jnp.dot(wide[at, :], shard, preferred_element_type=jnp.float32),
            )

    def chunk_rows(i):
        return pl.ds(i * CHUNK, CHUNK)

    def to_sibling(which, i):
        at = chunk_rows(i)
        return remote(
            leaving.at[which, at], arriving.at[which, at],
            sib_send.at[4 * which + i], sib_recv.at[4 * which + i], sibling,
        )

    def for_sibling(which, y):
        def put(at, value):
            leaving[which, at, :] = value.astype(jnp.bfloat16)

        for i in range(chunks):
            product(2 * y + 1 - core, put, i, i + 1)
            to_sibling(which, i).start()

    def keep(which, y, i):
        def put(at, value):
            own[at, :] = value

        product(2 * y + core, put, i, i + 1)
        to_sibling(which, i).wait_recv()

    def far_copy(i):
        at = chunk_rows(i)
        return remote(far_out.at[at], far_in.at[at], far_sem.at[i], far_sem.at[4 + i], opposite)

    units[0].begin()
    units[2].begin()
    units[0].send_line(0, 0)
    held[:, group_rows(context)] = ours[:, y_lo, :, column_of(context)]
    gated_ref[context] = gated_group[context]
    for n in range(HALF):
        fgrad_ref[:, n * INNER : (n + 1) * INNER] = fields[2, n]
    leave(3).start()

    @pl.loop(0, 16)
    def _(i):
        ref = plane.at[core, i]
        remote(ref, ref, spread_send.at[0], spread_recv.at[i], sibling).wait_recv()

    plane_pair.start()
    ours_across.wait_recv()
    units[1].begin()
    units[3].begin()
    for unit in units[1:]:
        unit.send_line(0, 0)
    for unit in units[:2]:
        unit.relay()
        unit.lines()
    for unit in units[2:]:
        unit.relay()

    @pl.loop(1, 32)
    def _(i):
        back_arrival(i).wait_recv()

    for_sibling(0, 1 - y_hi)
    for unit in units[:2]:
        unit.pass_line(0, 0)
        unit.last_line()
    for i in range(chunks):
        keep(0, 1 - y_hi, i)
        at = chunk_rows(i)
        far_out[at, :] = (own[at, :] + arriving[0, at, :].astype(jnp.float32)).astype(jnp.bfloat16)
        far_copy(i).start()
    for unit in units[2:]:
        unit.lines()
    for unit in units[:2]:
        unit.pass_line(1, -1)
        unit.pass_line(2, 1)
    for unit in units[2:]:
        unit.pass_line(0, 0)
        unit.last_line()
    for unit in units[:2]:
        unit.pass_line(3, 2)

    @pl.loop(1, 32)
    def _(i):
        gated_copy(i).start()

    for unit in units[2:]:
        unit.pass_line(1, -1)
        unit.pass_line(2, 1)
    for_sibling(1, y_hi)
    for unit in units[2:]:
        unit.pass_line(3, 2)
    plane_pair.wait_recv()
    for unit in units[:2]:
        unit.end()
    weight_send(0)
    for i in range(chunks):
        keep(1, y_hi, i)
        at = chunk_rows(i)
        own[at, :] += arriving[1, at, :].astype(jnp.float32)

    @pl.loop(1, 32)
    def _(i):
        cot_copy(i).wait_send()
        proj_copy(i).wait_send()
        back_copy(i).wait_send()
        gated_copy(i).wait()

    leave(0).start()
    for copy in pieces + passed + [token_pair, plane_pair, ours_across]:
        copy.wait_send()
    spread_done(0, dp)
    spread_done(1, far)
    for unit in units[2:]:
        unit.end()
    weight_send(1)
    weight_end(0)
    for i in range(chunks):
        far_copy(i).wait_recv()
        at = chunk_rows(i)
        tgrad_ref[:, i * CHUNK : (i + 1) * CHUNK] = (
            (own[at, :] + far_in[at, :].astype(jnp.float32)).T.astype(jnp.bfloat16)
        )
    leave(1).start()
    for unit in units:
        for copy in unit.started:
            copy.wait_send()
    for i in range(chunks):
        far_copy(i).wait_send()
        for which in range(2):
            to_sibling(which, i).wait_send()
    for i in range(2):
        weight_copy(i).wait_send()
    weight_end(1)
    wgrad_ref[...] = wgrad_rows[...].astype(jnp.bfloat16)
    leave(2).start()
    for i in range(4):
        leave(i).wait()


def finish_kernel(*refs):
    sources, targets, held, sem = refs[:4], refs[4:8], refs[8:12], refs[12]
    arrive = [pltpu.make_async_copy(a, b, sem.at[i]) for i, (a, b) in enumerate(zip(sources, held))]
    depart = [pltpu.make_async_copy(a, b, sem.at[4 + i]) for i, (a, b) in enumerate(zip(held, targets))]
    for copy in arrive:
        copy.start()
    for first, second in zip(arrive, depart):
        first.wait()
        second.start()
    for copy in depart:
        copy.wait()


def finished(*arrays):
    hbm = pl.BlockSpec(memory_space=pl.ANY)
    return pl.pallas_call(
        finish_kernel,
        out_shape=tuple(jax.ShapeDtypeStruct(array.shape, array.dtype) for array in arrays),
        in_specs=[hbm] * 4,
        out_specs=[hbm] * 4,
        scratch_shapes=[pltpu.VMEM(array.shape, array.dtype) for array in arrays]
        + [pltpu.SemaphoreType.DMA((8,))],
        compiler_params=pltpu.CompilerParams(vmem_limit_bytes=56 * 1024 * 1024),
        name="results",
    )(*arrays)


def on_device(tokens, in_weight, short_taps, filters, cotangent):
    channels, length = filters.shape
    groups = lax.axis_size("context")
    rows, part = tokens.shape
    depth, streams, slab = in_weight.shape
    tiles = slab // INNER
    flat = (
        in_weight.reshape(depth, streams, tiles, INNER)
        .transpose(0, 2, 1, 3)
        .reshape(depth * streams * tiles, INNER)
    )
    taps = lax.dynamic_slice_in_dim(short_taps, lax.axis_index("context") * channels, channels, axis=2)
    taps = jnp.broadcast_to(taps[..., None], taps.shape + (INNER,))
    matrices, turns = tables()
    vmem = pl.BlockSpec(memory_space=pltpu.VMEM)
    hbm = pl.BlockSpec(memory_space=pl.ANY)

    def bf16(*shape):
        return pltpu.VMEM(shape, jnp.bfloat16)

    def f32(*shape):
        return pltpu.VMEM(shape, jnp.float32)

    def dma(*counts):
        return [pltpu.SemaphoreType.DMA((count,)) for count in counts]

    size = ROWS * channels
    results = pl.pallas_call(
        block_kernel,
        out_shape=(
            jax.ShapeDtypeStruct((groups, channels, rows), jnp.bfloat16),
            jax.ShapeDtypeStruct((rows, part), jnp.bfloat16),
            jax.ShapeDtypeStruct((256 * streams * tiles, INNER), jnp.bfloat16),
            jax.ShapeDtypeStruct((channels, length), jnp.float32),
        ),
        in_specs=[hbm, hbm, hbm, vmem, hbm, hbm, hbm],
        out_specs=[hbm] * 4,
        scratch_shapes=[
            f32(channels, length),
            bf16(*matrices.shape),
            f32(*turns.shape),
            bf16(groups, channels, rows),
            bf16(rows, part),
            bf16(256 * streams * tiles, INNER),
            f32(256 * streams * tiles, INNER),
            f32(channels, length),
            *dma(4),
            bf16(4, CHUNK * 8, INNER),
            f32(CHUNK * 8, INNER),
            bf16(depth, streams * slab),
            bf16(4, rows, part),
            bf16(streams, groups, channels, rows),
            f32(rows, streams * slab),
            bf16(2, 16, rows, 256),
            bf16(groups, streams, channels, rows),
            bf16(groups, channels, rows),
            f32(3, HALF, channels, INNER),
            f32(3, size, 2 * INNER),
            f32(3, size, 2 * INNER),
            f32(HALF, channels, INNER),
            bf16(groups, channels, rows),
            bf16(streams, 2, channels, length // 2),
            bf16(streams, slab, length // 2),
            bf16(streams, slab, rows),
            f32(streams, slab, 256),
            bf16(2, part, rows),
            bf16(2, part, rows),
            bf16(part, rows),
            bf16(part, rows),
            f32(part, rows),
            bf16(streams, slab, 256),
            bf16(streams, slab, 256),
            *dma(4, 5, 2, PIECES, PIECES, PIECES, PIECES, 16, 16, 4, 32, 32, 32, 32),
            *dma(32, 32, 32, 32, 8, 8, 8, 80, 80, 2, 2),
        ],
        compiler_params=pltpu.CompilerParams(
            collective_id=0, has_side_effects=True, vmem_limit_bytes=56 * 1024 * 1024
        ),
        cost_estimate=pl.CostEstimate(
            flops=8_000_000_000, bytes_accessed=24_000_000, transcendentals=0
        ),
        name="block_forward_backward",
    )(
        tokens, cotangent.reshape(groups, channels, rows), filters, taps,
        jnp.asarray(matrices), jnp.asarray(turns), flat,
    )
    gated_out, token_grad, weight_grad, filter_grad = finished(*results)
    weight_grad = weight_grad.reshape(256, tiles, streams, INNER).transpose(0, 2, 1, 3)
    return (
        gated_out.reshape(slab, rows),
        token_grad,
        weight_grad.reshape(256, streams, slab),
        filter_grad,
    )


def solution(mesh):
    placed = (
        P("context", "dp"),
        P(None, None, "dp"),
        P(None, None, "dp"),
        P(("dp", "context"), None),
        P("dp", "context"),
    )
    return jax.shard_map(
        on_device,
        mesh=mesh,
        in_specs=placed,
        out_specs=(
            P("dp", "context"),
            P("context", "dp"),
            P("context", None, "dp"),
            P(("dp", "context"), None),
        ),
        check_vma=False,
    )
```

```python
import functools
import math

import jax
import jax.numpy as jnp
import numpy as np
from jax import lax
from jax.experimental import pallas as pl
from jax.experimental.pallas import tpu as pltpu
from jax.sharding import PartitionSpec as P

OUTER = 64
INNER = 128
TOTAL = OUTER * INNER
HALF = OUTER // 2
KEPT = [0, 8, 16, 24, 32] + [k1 + 8 * k2 for k1 in (1, 2, 3) for k2 in range(8)] + [4, 12, 20, 28]
ROWS = len(KEPT)


def add(a, b):
    return b if a is None else a if b is None else a + b


def neg(a):
    return None if a is None else -a


def sub(a, b):
    return a if b is None else neg(b) if a is None else a - b


def scaled(a, factor):
    if a is None or abs(factor) < 1e-12:
        return None
    if abs(factor - 1) < 1e-12:
        return a
    if abs(factor + 1) < 1e-12:
        return -a
    return a * np.float32(factor)


def cadd(a, b):
    return (add(a[0], b[0]), add(a[1], b[1]))


def csub(a, b):
    return (sub(a[0], b[0]), sub(a[1], b[1]))


def turned(a, step, count):
    step %= count
    if (8 * step) % count == 0 and (8 * step // count) % 2 == 1:
        eighth = 8 * step // count
        root = math.sqrt(0.5)
        re, im = a
        if eighth == 1:
            pair = (sub(re, im), add(re, im))
        elif eighth == 3:
            pair = (neg(add(re, im)), sub(re, im))
        elif eighth == 5:
            pair = (sub(im, re), neg(add(re, im)))
        else:
            pair = (add(re, im), sub(im, re))
        return (scaled(pair[0], root), scaled(pair[1], root))
    angle = 2 * math.pi * step / count
    cos, sin = math.cos(angle), math.sin(angle)
    return (
        sub(scaled(a[0], cos), scaled(a[1], sin)),
        add(scaled(a[0], sin), scaled(a[1], cos)),
    )


def dft(values, sign):
    count = len(values)
    if count == 1:
        return values
    even = dft(values[0::2], sign)
    odd = dft(values[1::2], sign)
    odd = [turned(entry, sign * index, count) for index, entry in enumerate(odd)]
    return [cadd(a, b) for a, b in zip(even, odd)] + [csub(a, b) for a, b in zip(even, odd)]


def outer_forward(load):
    parts = []
    for second in range(8):
        line = [(load(8 * first + second), None) if first < 4 else (None, None) for first in range(8)]
        parts.append(dft(line, -1)[:5])
    results = []
    for first in (0, 1, 2, 3, 4):
        line = [turned(parts[second][first], -second * first, OUTER) for second in range(8)]
        full = dft(line, -1)
        results += {0: full[:5], 4: full[:4]}.get(first, full)
    return results


def real_line(values, count):
    top = values[0][0]
    last = values[4][0]
    a = add(top, last)
    b = sub(top, last)
    (r1, i1), (r2, i2), (r3, i3) = values[1:4]
    s13, d13 = add(r1, r3), sub(r1, r3)
    si, di = add(i1, i3), sub(i1, i3)
    root = math.sqrt(0.5)
    p = scaled(sub(d13, si), root)
    q = scaled(add(d13, si), root)
    out = [
        add(add(a, r2), s13),
        add(sub(b, i2), p),
        sub(sub(a, r2), di),
        sub(add(b, i2), q),
    ]
    if count > 4:
        out += [
            sub(add(a, r2), s13),
            sub(sub(b, i2), p),
            add(sub(a, r2), di),
            add(add(b, i2), q),
        ]
    return out


def outer_inverse(load):
    zero = real_line([load(row) for row in range(5)], 8)
    lines = []
    for first in (1, 2, 3):
        line = dft([load(5 + 8 * (first - 1) + second) for second in range(8)], 1)
        lines.append([turned(line[second], second * first, OUTER) for second in range(8)])
    tail = dft([load(29 + second) if second < 4 else (None, None) for second in range(8)], 1)
    tail = [turned(tail[second], second, 16)[0] for second in range(8)]
    results = [None] * HALF
    for second in range(8):
        line = [(zero[second], None)] + [lines[first][second] for first in range(3)] + [(tail[second], None)]
        for first, entry in enumerate(real_line(line, 4)):
            results[8 * first + second] = entry
    return results


def tables():
    index = np.arange(INNER, dtype=np.float64)
    angle = 2 * np.pi / INNER * (np.outer(index, index) % INNER)
    cos, sin = np.cos(angle), np.sin(angle)
    wide = np.block([[cos, -sin], [sin, cos]])
    high = wide.astype(jnp.bfloat16)
    low = (wide - high.astype(np.float64)).astype(jnp.bfloat16)
    inverse = wide.T
    inverse_high = inverse.astype(jnp.bfloat16)
    inverse_low = (inverse - inverse_high.astype(np.float64)).astype(jnp.bfloat16)
    matrices = np.stack([high, low, inverse_high, inverse_low])
    turn = 2 * np.pi / TOTAL * np.outer(np.array(KEPT, np.float64), index)
    weight = np.array([1.0 if k in (0, HALF) else 2.0 for k in KEPT])[:, None] / TOTAL
    turns = np.stack([np.cos(turn), np.sin(turn), weight * np.cos(turn), weight * np.sin(turn)])
    return matrices, turns.astype(np.float32)


def times_matrix(wide, high, low):
    top = wide.astype(jnp.bfloat16)
    rest = (wide - top.astype(jnp.float32)).astype(jnp.bfloat16)
    dot = functools.partial(jnp.dot, preferred_element_type=jnp.float32)
    return dot(top, high) + (dot(rest, high) + dot(top, low))


def lagged(here, before, lag):
    lane = lax.broadcasted_iota(jnp.int32, here.shape, here.ndim - 1)
    rolled = pltpu.roll(here, lag, here.ndim - 1)
    if before is None:
        return jnp.where(lane < lag, 0.0, rolled)
    return jnp.where(lane < lag, pltpu.roll(before, lag, here.ndim - 1), rolled)


def led(here, after, lead):
    lane = lax.broadcasted_iota(jnp.int32, here.shape, here.ndim - 1)
    width = here.shape[-1]
    rolled = pltpu.roll(here, width - lead, here.ndim - 1)
    if after is None:
        return jnp.where(lane >= width - lead, 0.0, rolled)
    return jnp.where(lane >= width - lead, pltpu.roll(after, width - lead, here.ndim - 1), rolled)


MESH = pl.DeviceIdType.MESH
CHUNK = 512
PIECES = 4


def coords():
    dp = lax.axis_index("dp")
    context = lax.axis_index("context")
    return dp // 2, dp % 2, context // 8, (context // 2) % 4, context % 2


def device(y_hi, core, z, x, y_lo):
    return (y_hi * 2 + core, z * 8 + x * 2 + y_lo)


def greet(partner):
    pl.semaphore_signal(
        pltpu.get_barrier_semaphore(), inc=1, device_id=partner, device_id_type=MESH
    )


def remote(src, dst, send_sem, recv_sem, partner):
    return pltpu.make_async_remote_copy(
        src_ref=src,
        dst_ref=dst,
        send_sem=send_sem,
        recv_sem=recv_sem,
        device_id=partner,
        device_id_type=MESH,
    )


def greet_line():
    dp = lax.axis_index("dp")
    context = lax.axis_index("context")

    @pl.loop(1, 32)
    def _(i):
        greet((dp, lax.rem(context + i, 32)))

    @pl.loop(1, 4)
    def _(i):
        greet((lax.rem(dp + i, 4), context))


def block_kernel(
    tok_ref, cot_ref, filt_hbm, taps_hbm, mat_hbm, turn_hbm, flat_ref,
    gated_hbm, tgrad_hbm, wgrad_hbm, fgrad_hbm,
    filt_ref, mat_ref, turn_ref, taps_all, taps_ref, gated_ref, tgrad_ref, wgrad_ref, wgrad_rows, fgrad_ref, out_sem,
    stage, loose, wide, gathered, outgoing, total, plane, proj, cot,
    fields, spec, prod, gate_ref, gated_group,
    ours, blocks, held, mixed, sums, leaving, arriving, far_out, far_in, own, swap_out, swap_in,
    load_sem, in_sem, pair_sem, half_send, half_recv, pass_send, pass_recv,
    spread_send, spread_recv, plane_sem, proj_send, proj_recv, cot_send, cot_recv,
    back_send, back_recv, gated_send, gated_recv, sib_send, sib_recv, far_sem,
    ring_send, ring_recv, swap_send, swap_recv,
):
    y_hi, core, z, x, y_lo = coords()
    dp = lax.axis_index("dp")
    context = lax.axis_index("context")
    rows, part = tok_ref.shape
    channels = filt_hbm.shape[0]
    size = ROWS * channels
    sibling = device(y_hi, 1 - core, z, x, y_lo)
    opposite = device(1 - y_hi, core, z, x, y_lo)
    slot = z * 4 + x
    chunks = part // CHUNK
    flat_rows = CHUNK * 8

    def quarter(j):
        return 2 * lax.rem(y_hi + j // 2, 2) + lax.rem(core + j % 2, 2)

    def chunk_of(step):
        return quarter(step // chunks) * chunks + step % chunks

    def load(step):
        at = pl.ds(pl.multiple_of(chunk_of(step) * flat_rows, flat_rows), flat_rows)
        return pltpu.make_async_copy(flat_ref.at[at], stage.at[step % 4], load_sem.at[step % 4])

    def cot_copy(i):
        to = lax.rem(context + i, 32)
        return remote(cot_ref.at[to], cot.at[context], cot_send.at[i], cot_recv.at[i], (dp, to))

    def separate(first, last, sends=False):
        @pl.loop(first, last)
        def _(step):
            load(step).wait()
            loose[...] = stage[step % 4].astype(jnp.float32)
            at = pl.ds(pl.multiple_of(chunk_of(step) * CHUNK, CHUNK), CHUNK)
            for stream in range(2):
                for tile in range(4):
                    column = stream * 512 + tile * INNER
                    wide[at, column : column + INNER] = loose[
                        pl.ds(2 * tile + stream, CHUNK, stride=8), :
                    ].astype(jnp.bfloat16)

            @pl.when(step + 4 < 4 * chunks)
            def _():
                load(step + 4).start()

            for j in range(4 if sends else 0):
                to = 1 + (step - first) * 4 + j

                @pl.when(to < 32)
                def _():
                    cot_copy(to).start()

    def multiply(j, first, last):
        for piece in range(first, last):
            at = pl.ds(pl.multiple_of((quarter(j) * chunks + piece) * CHUNK, CHUNK), CHUNK)
            total[...] += jnp.dot(
                gathered[quarter(j), :, piece * CHUNK : (piece + 1) * CHUNK],
                wide[at, :],
                preferred_element_type=jnp.float32,
            )

    own_tokens = pltpu.make_async_copy(tok_ref, gathered.at[dp], in_sem.at[0])
    own_cot = pltpu.make_async_copy(cot_ref.at[context], cot.at[context], in_sem.at[1])
    own_tables = [
        pltpu.make_async_copy(src, dst, in_sem.at[2 + i])
        for i, (src, dst) in enumerate(((filt_hbm, filt_ref), (mat_hbm, mat_ref), (turn_hbm, turn_ref), (taps_hbm, taps_all)))
    ]
    for step in range(4):
        load(step).start()
    own_tokens.start()
    own_cot.start()
    for copy in own_tables:
        copy.start()
    greet_line()

    @pl.loop(1, 16)
    def _(i):
        other = lax.rem(slot + i, 16)
        greet(device(y_hi, 1 - core, other // 4, other % 4, y_lo))

    separate(0, 3)
    pl.semaphore_wait(pltpu.get_barrier_semaphore(), 34 + 15)

    width = part // PIECES
    pieces = [
        remote(
            tok_ref.at[:, i * width : (i + 1) * width],
            gathered.at[dp, :, i * width : (i + 1) * width],
            half_send.at[i], half_recv.at[i], opposite,
        )
        for i in range(PIECES)
    ]
    token_pair = remote(tok_ref, gathered.at[dp], pair_sem.at[0], pair_sem.at[1], sibling)
    pieces[0].start()
    token_pair.start()
    for copy in pieces[1:]:
        copy.start()
    own_tokens.wait()
    far = 2 * (1 - y_hi) + core
    passed = [
        remote(
            gathered.at[far, :, i * width : (i + 1) * width],
            gathered.at[far, :, i * width : (i + 1) * width],
            pass_send.at[i], pass_recv.at[i], sibling,
        )
        for i in range(PIECES)
    ]

    def spread(which, i, block):
        to_x = i // 2
        to_core = i % 2
        column = pl.multiple_of(512 * to_x + 256 * to_core, 256)
        src = gathered.at[block, :, pl.ds(column, 256)]
        here = (block == z) & (to_x == x) & (to_core == core)
        there = remote(
            src, plane.at[to_core, slot], spread_send.at[which * 8 + i], spread_recv.at[slot],
            device(y_hi, to_core, block, to_x, y_lo),
        )
        return here, there, src

    def spread_start(which, block, first, last):
        @pl.loop(first, last)
        def _(i):
            here, there, src = spread(which, i, block)

            @pl.when(here)
            def _():
                pltpu.make_async_copy(src, plane.at[core, slot], spread_recv.at[slot]).start()

            @pl.when(jnp.logical_not(here))
            def _():
                there.start()

    def spread_done(which, block):
        @pl.loop(0, 8)
        def _(i):
            here, there, _src = spread(which, i, block)

            @pl.when(jnp.logical_not(here))
            def _():
                there.wait_send()

    across = device(y_hi, core, z, x, 1 - y_lo)
    plane_pair = remote(plane.at[core], plane.at[core], plane_sem.at[0], plane_sem.at[1], sibling)

    spread_start(0, dp, 0, 8)

    total[...] = jnp.zeros_like(total)
    separate(3, 11, True)
    multiply(0, 0, 4)
    token_pair.wait_recv()
    for i in range(PIECES):
        if i < 3:
            pieces[i].wait_recv()
            passed[i].start()
            spread_start(1, far, 2 * i, 2 * i + 2)
            separate(11 + i, 12 + i)
        else:
            separate(14, 16)
            multiply(1, 0, 4)
            multiply(2, 0, 3)
            for n in range(3):
                passed[n].wait_recv()
                multiply(3, n, n + 1)
            pieces[i].wait_recv()
            passed[i].start()
            multiply(2, 3, 4)
            passed[3].wait_recv()
            multiply(3, 3, 4)
    def transform(begin, end):
        @pl.loop(begin, end)
        def _(which):
            for row, (re, im) in enumerate(outer_forward(lambda n: fields[which, n])):
                cos = turn_ref[0, row][None, :]
                sin = turn_ref[1, row][None, :]
                at = pl.ds(row * channels, channels)
                if im is None:
                    spec[which, at, :INNER] = re * cos
                    spec[which, at, INNER:] = -(re * sin)
                else:
                    spec[which, at, :INNER] = re * cos + im * sin
                    spec[which, at, INNER:] = im * cos - re * sin
            spec[which] = times_matrix(spec[which], mat_ref[0], mat_ref[1])

    outgoing[...] = total[...].T.astype(jnp.bfloat16).reshape(outgoing.shape)

    def proj_copy(i):
        to = lax.rem(context + i, 32)
        return remote(outgoing.at[:, to], proj.at[context], proj_send.at[i], proj_recv.at[i], (dp, to))

    @pl.loop(1, 32)
    def _(i):
        proj_copy(i).start()

    proj[context] = outgoing[:, context]
    spread_start(1, far, 6, 8)
    for copy in own_tables:
        copy.wait()

    tile = pl.ds(pl.multiple_of(context // 8 * INNER, INNER), INNER)
    lane = lax.broadcasted_iota(jnp.int32, (channels, INNER), 1)
    picked = lane == context % 8 * channels + lax.broadcasted_iota(jnp.int32, (channels, INNER), 0)
    for stream in range(2):
        for lag in range(3):
            line = taps_all[lag, pl.ds(stream, 1), tile]
            column = jnp.sum(jnp.where(picked, line, 0.0), axis=1, keepdims=True)
            taps_ref[stream, lag] = jnp.broadcast_to(column, (channels, INNER))
    for n in range(HALF):
        fields[0, n] = filt_ref[:, n * INNER : (n + 1) * INNER]

    @pl.loop(1, 32)
    def _(i):
        cot_copy(i).wait_recv()

    own_cot.wait()

    @pl.loop(1, 32)
    def _(i):
        proj_copy(i).wait_recv()

    def short(stream, n):
        here = proj[n, stream].astype(jnp.float32)
        before = proj[n - 1, stream].astype(jnp.float32) if n else None
        result = taps_ref[stream, 0] * here
        for lag in (1, 2):
            result = result + taps_ref[stream, lag] * lagged(here, before, lag)
        return result

    for n in range(HALF):
        gate = short(0, n)
        gate_ref[n] = gate
        fields[2, n] = cot[n].astype(jnp.float32) * gate
        fields[1, n] = short(1, n)

    transform(0, 3)

    @pl.loop(0, ROWS)
    def _(row):
        at = pl.ds(pl.multiple_of(row * channels, channels), channels)
        (hr, hi), (vr, vi), (gr, gi) = [
            (spec[which, at, :INNER], spec[which, at, INNER:]) for which in range(3)
        ]

        def put(which, re, im):
            prod[which, at, :INNER] = re
            prod[which, at, INNER:] = im

        put(0, hr * vr - hi * vi, hr * vi + hi * vr)
        put(1, hr * gr + hi * gi, hr * gi - hi * gr)
        put(2, vr * gr + vi * gi, vr * gi - vi * gr)

    @pl.loop(0, 3)
    def _(which):
        prod[which] = times_matrix(prod[which], mat_ref[2], mat_ref[3])

        def turned_row(row):
            cos = turn_ref[2, row][None, :]
            sin = turn_ref[3, row][None, :]
            at = pl.ds(row * channels, channels)
            re, im = prod[which, at, :INNER], prod[which, at, INNER:]
            return re * cos - im * sin, im * cos + re * sin

        for n, entry in enumerate(outer_inverse(turned_row)):
            fields[which, n] = entry

    for n in range(HALF):
        entry = fields[0, n]
        gated_group[n] = (gate_ref[n] * entry).astype(jnp.bfloat16)
        gate_ref[n] = cot[n].astype(jnp.float32) * entry

    for stream, load_row in enumerate((lambda n: gate_ref[n], lambda n: fields[1, n])):
        for n in range(HALF):
            here = load_row(n)
            after = load_row(n + 1) if n + 1 < HALF else None
            result = taps_ref[stream, 0] * here
            for lead in (1, 2):
                result = result + taps_ref[stream, lead] * led(here, after, lead)
            column = n // 2 * INNER
            ours[stream, n % 2, :, column : column + INNER] = result.astype(jnp.bfloat16)

    def group_rows(group):
        return pl.ds(pl.multiple_of(group * channels, channels), channels)

    def column_of(index):
        return pl.ds(pl.multiple_of(index // 2 * INNER, INNER), INNER)

    def back_copy(i):
        to = lax.rem(context + i, 32)
        return remote(
            ours.at[:, to % 2, :, column_of(to)], held.at[:, group_rows(context)],
            back_send.at[i], back_recv.at[i], (dp, to),
        )

    def back_arrival(i):
        source = lax.rem(context + 32 - i, 32)
        return remote(
            ours.at[:, source % 2, :, column_of(source)], held.at[:, group_rows(source)],
            back_send.at[i], back_recv.at[i], (dp, source),
        )

    ours_across = remote(
        ours.at[:, 1 - y_lo], blocks.at[:, slot, y_lo], plane_sem.at[2], plane_sem.at[3], across
    )

    def gated_copy(i):
        to = lax.rem(context + i, 32)
        return remote(
            gated_group.at[to], gated_ref.at[context], gated_send.at[i], gated_recv.at[i], (dp, to)
        )

    def leave(which):
        src, dst = (
            (gated_ref, gated_hbm), (tgrad_ref, tgrad_hbm), (wgrad_ref, wgrad_hbm), (fgrad_ref, fgrad_hbm),
        )[which]
        return pltpu.make_async_copy(src, dst, out_sem.at[which])

    @pl.loop(1, 32)
    def _(i):
        back_copy(i).start()

    ours_across.start()
    blocks[:, slot, y_lo] = ours[:, y_lo]

    def place(first, along, aside):
        if first == "x":
            return lax.rem(z + aside + 4, 4) * 4 + lax.rem(x + along + 4, 4)
        return lax.rem(z + along + 4, 4) * 4 + lax.rem(x + aside + 4, 4)

    def neighbour(first, along, aside):
        at = place(first, along, aside)
        return device(y_hi, core, at // 4, at % 4, y_lo)

    class Unit:
        def __init__(self, number):
            self.stream = number // 2
            self.from_y = (y_lo, 1 - y_lo)[number % 2]
            self.first = ("x", "z")[number % 2]
            self.base = 20 * number
            self.started = []

        def copy(self, index, along, aside, part, step_along, step_aside):
            begin, count = {None: (0, 2048), 0: (0, 1024), 1: (1024, 1024)}[part]
            ref = blocks.at[
                self.stream,
                place(self.first, along, aside),
                self.from_y,
                :,
                pl.ds(begin, count),
            ]
            return remote(
                ref, ref, ring_send.at[self.base + index], ring_recv.at[self.base + index],
                neighbour(self.first, step_along, step_aside),
            )

        def send(self, *args):
            copy = self.copy(*args)
            copy.start()
            self.started.append(copy)

        def arrived(self, index, along, aside, part):
            self.copy(index, along, aside, part, 1, 0).wait_recv()

        def send_line(self, which, along):
            self.send(4 + 4 * which, along, 0, None, 0, 1)
            self.send(5 + 4 * which, along, 0, None, 0, -1)

        def pass_line(self, which, along):
            self.arrived(4 + 4 * which, along, -1, None)
            self.send(6 + 4 * which, along, -1, 0, 0, 1)
            self.arrived(5 + 4 * which, along, 1, None)
            self.send(7 + 4 * which, along, 1, 1, 0, -1)

        def begin(self):
            self.send(0, 0, 0, None, 1, 0)
            self.send(1, 0, 0, None, -1, 0)

        def relay(self):
            self.arrived(0, -1, 0, None)
            self.send(2, -1, 0, 0, 1, 0)
            self.arrived(1, 1, 0, None)
            self.send(3, 1, 0, 1, -1, 0)

        def lines(self):
            self.send_line(1, -1)
            self.send_line(2, 1)

        def last_line(self):
            self.arrived(2, -2, 0, 0)
            self.arrived(3, 2, 0, 1)
            self.send_line(3, 2)

        def end(self):
            for which, along in enumerate((0, -1, 1, 2)):
                self.arrived(6 + 4 * which, along, -2, 0)
                self.arrived(7 + 4 * which, along, 2, 1)

    units = [Unit(number) for number in range(4)]

    def weight_copy(which):
        return remote(
            swap_out.at[which], swap_in.at[which], swap_send.at[which], swap_recv.at[which], across
        )

    def weight_sum(which, half):
        return jnp.dot(
            blocks[which // 2, :, (y_lo, 1 - y_lo)[which % 2]].reshape(256, 16 * INNER),
            plane[half].reshape(16 * INNER, 256),
            preferred_element_type=jnp.float32,
        )

    def weight_send(which):
        swap_out[which] = weight_sum(which, 1 - y_lo).astype(jnp.bfloat16)
        weight_copy(which).start()

    def weight_own(which):
        sums[which] = weight_sum(which, y_lo)

    def weight_end(stream):
        for mine, theirs in ((2 * stream + 1, 2 * stream), (2 * stream, 2 * stream + 1)):
            weight_copy(theirs).wait_recv()
            value = sums[mine] + swap_in[theirs].astype(jnp.float32)
            mixed[:, (y_lo, 1 - y_lo)[mine % 2]] = value.reshape(16, channels, 256)
        turned_sum = mixed[...].reshape(512, 256).T
        for tile in range(4):
            wgrad_rows[pl.ds(2 * tile + stream, 256, stride=8), :] = turned_sum[
                :, tile * INNER : (tile + 1) * INNER
            ]

    def product(q, put, first, last):
        shard = held[...].reshape(1024, INNER)
        for i in range(first, last):
            at = pl.ds(pl.multiple_of(q * part + i * CHUNK, CHUNK), CHUNK)
            put(
                pl.ds(i * CHUNK, CHUNK),
                jnp.dot(wide[at, :], shard, preferred_element_type=jnp.float32),
            )

    def chunk_rows(i):
        return pl.ds(i * CHUNK, CHUNK)

    def to_sibling(which, i):
        at = chunk_rows(i)
        return remote(
            leaving.at[which, at], arriving.at[which, at],
            sib_send.at[4 * which + i], sib_recv.at[4 * which + i], sibling,
        )

    def for_sibling(which, y):
        def put(at, value):
            leaving[which, at, :] = value.astype(jnp.bfloat16)

        for i in range(chunks):
            product(2 * y + 1 - core, put, i, i + 1)
            to_sibling(which, i).start()

    def keep(which, y, i):
        def put(at, value):
            own[at, :] = value

        product(2 * y + core, put, i, i + 1)
        to_sibling(which, i).wait_recv()

    def far_copy(i):
        at = chunk_rows(i)
        return remote(far_out.at[at], far_in.at[at], far_sem.at[i], far_sem.at[4 + i], opposite)

    units[0].begin()
    units[2].begin()
    units[0].send_line(0, 0)
    held[:, group_rows(context)] = ours[:, y_lo, :, column_of(context)]
    gated_ref[context] = gated_group[context]
    for n in range(HALF):
        fgrad_ref[:, n * INNER : (n + 1) * INNER] = fields[2, n]
    leave(3).start()

    @pl.loop(0, 16)
    def _(i):
        ref = plane.at[core, i]
        remote(ref, ref, spread_send.at[0], spread_recv.at[i], sibling).wait_recv()

    plane_pair.start()
    ours_across.wait_recv()
    units[1].begin()
    units[3].begin()
    for unit in units[1:]:
        unit.send_line(0, 0)
    for unit in units[:2]:
        unit.relay()
        unit.lines()
    for unit in units[2:]:
        unit.relay()

    @pl.loop(1, 32)
    def _(i):
        back_arrival(i).wait_recv()

    for_sibling(0, 1 - y_hi)
    for unit in units[:2]:
        unit.pass_line(0, 0)
        unit.last_line()
    for i in range(chunks):
        keep(0, 1 - y_hi, i)
        at = chunk_rows(i)
        far_out[at, :] = (own[at, :] + arriving[0, at, :].astype(jnp.float32)).astype(jnp.bfloat16)
        far_copy(i).start()
    for unit in units[2:]:
        unit.lines()
    for unit in units[:2]:
        unit.pass_line(1, -1)
        unit.pass_line(2, 1)
    for unit in units[2:]:
        unit.pass_line(0, 0)
        unit.last_line()
    for unit in units[:2]:
        unit.pass_line(3, 2)

    @pl.loop(1, 32)
    def _(i):
        gated_copy(i).start()

    for unit in units[2:]:
        unit.pass_line(1, -1)
        unit.pass_line(2, 1)
    for_sibling(1, y_hi)
    for unit in units[2:]:
        unit.pass_line(3, 2)
    plane_pair.wait_recv()
    for i in range(2):
        units[i].end()
        weight_send(i)
    for i in range(chunks):
        keep(1, y_hi, i)
        at = chunk_rows(i)
        own[at, :] += arriving[1, at, :].astype(jnp.float32)

    @pl.loop(1, 32)
    def _(i):
        cot_copy(i).wait_send()
        proj_copy(i).wait_send()
        back_copy(i).wait_send()
        gated_copy(i).wait()

    leave(0).start()
    for copy in pieces + passed + [token_pair, plane_pair, ours_across]:
        copy.wait_send()
    spread_done(0, dp)
    spread_done(1, far)
    weight_own(0)
    weight_own(1)
    for i in range(2, 4):
        units[i].end()
        weight_send(i)
    weight_own(2)
    weight_own(3)
    weight_end(0)
    for i in range(chunks):
        far_copy(i).wait_recv()
        at = chunk_rows(i)
        tgrad_ref[:, i * CHUNK : (i + 1) * CHUNK] = (
            (own[at, :] + far_in[at, :].astype(jnp.float32)).T.astype(jnp.bfloat16)
        )
    leave(1).start()
    for unit in units:
        for copy in unit.started:
            copy.wait_send()
    for i in range(chunks):
        far_copy(i).wait_send()
        for which in range(2):
            to_sibling(which, i).wait_send()
    for i in range(4):
        weight_copy(i).wait_send()
    weight_end(1)
    wgrad_ref[...] = wgrad_rows[...].astype(jnp.bfloat16)
    leave(2).start()
    for i in range(4):
        leave(i).wait()


def finish_kernel(*refs):
    sources, targets, held, sem = refs[:4], refs[4:8], refs[8:12], refs[12]
    arrive = [pltpu.make_async_copy(a, b, sem.at[i]) for i, (a, b) in enumerate(zip(sources, held))]
    depart = [pltpu.make_async_copy(a, b, sem.at[4 + i]) for i, (a, b) in enumerate(zip(held, targets))]
    for copy in arrive:
        copy.start()
    for first, second in zip(arrive, depart):
        first.wait()
        second.start()
    for copy in depart:
        copy.wait()


def finished(*arrays):
    hbm = pl.BlockSpec(memory_space=pl.ANY)
    return pl.pallas_call(
        finish_kernel,
        out_shape=tuple(jax.ShapeDtypeStruct(array.shape, array.dtype) for array in arrays),
        in_specs=[hbm] * 4,
        out_specs=[hbm] * 4,
        scratch_shapes=[pltpu.VMEM(array.shape, array.dtype) for array in arrays]
        + [pltpu.SemaphoreType.DMA((8,))],
        compiler_params=pltpu.CompilerParams(vmem_limit_bytes=56 * 1024 * 1024),
        name="results",
    )(*arrays)


def on_device(tokens, in_weight, short_taps, filters, cotangent):
    channels, length = filters.shape
    groups = lax.axis_size("context")
    rows, part = tokens.shape
    depth, streams, slab = in_weight.shape
    tiles = slab // INNER
    flat = (
        in_weight.reshape(depth, streams, tiles, INNER)
        .transpose(0, 2, 1, 3)
        .reshape(depth * streams * tiles, INNER)
    )
    matrices, turns = tables()
    hbm = pl.BlockSpec(memory_space=pl.ANY)

    def bf16(*shape):
        return pltpu.VMEM(shape, jnp.bfloat16)

    def f32(*shape):
        return pltpu.VMEM(shape, jnp.float32)

    def dma(*counts):
        return [pltpu.SemaphoreType.DMA((count,)) for count in counts]

    size = ROWS * channels
    results = pl.pallas_call(
        block_kernel,
        out_shape=(
            jax.ShapeDtypeStruct((groups, channels, rows), jnp.bfloat16),
            jax.ShapeDtypeStruct((rows, part), jnp.bfloat16),
            jax.ShapeDtypeStruct((256 * streams * tiles, INNER), jnp.bfloat16),
            jax.ShapeDtypeStruct((channels, length), jnp.float32),
        ),
        in_specs=[hbm] * 7,
        out_specs=[hbm] * 4,
        scratch_shapes=[
            f32(channels, length),
            bf16(*matrices.shape),
            f32(*turns.shape),
            f32(3, streams, slab),
            f32(streams, 3, channels, INNER),
            bf16(groups, channels, rows),
            bf16(rows, part),
            bf16(256 * streams * tiles, INNER),
            f32(256 * streams * tiles, INNER),
            f32(channels, length),
            *dma(4),
            bf16(4, CHUNK * 8, INNER),
            f32(CHUNK * 8, INNER),
            bf16(depth, streams * slab),
            bf16(4, rows, part),
            bf16(streams, groups, channels, rows),
            f32(rows, streams * slab),
            bf16(2, 16, rows, 256),
            bf16(groups, streams, channels, rows),
            bf16(groups, channels, rows),
            f32(3, HALF, channels, INNER),
            f32(3, size, 2 * INNER),
            f32(3, size, 2 * INNER),
            f32(HALF, channels, INNER),
            bf16(groups, channels, rows),
            bf16(streams, 2, channels, length // 2),
            bf16(streams, 16, 2, channels, length // 2),
            bf16(streams, slab, rows),
            f32(16, 2, channels, 256),
            f32(4, slab // 2, 256),
            bf16(2, part, rows),
            bf16(2, part, rows),
            bf16(part, rows),
            bf16(part, rows),
            f32(part, rows),
            bf16(4, slab // 2, 256),
            bf16(4, slab // 2, 256),
            *dma(4, 6, 2, PIECES, PIECES, PIECES, PIECES, 16, 16, 4, 32, 32, 32, 32),
            *dma(32, 32, 32, 32, 8, 8, 8, 80, 80, 4, 4),
        ],
        compiler_params=pltpu.CompilerParams(
            collective_id=0, has_side_effects=True, vmem_limit_bytes=56 * 1024 * 1024
        ),
        cost_estimate=pl.CostEstimate(
            flops=8_000_000_000, bytes_accessed=24_000_000, transcendentals=0
        ),
        name="block_forward_backward",
    )(
        tokens, cotangent.reshape(groups, channels, rows), filters, short_taps.transpose(1, 0, 2),
        jnp.asarray(matrices), jnp.asarray(turns), flat,
    )
    gated_out, token_grad, weight_grad, filter_grad = finished(*results)
    weight_grad = weight_grad.reshape(256, tiles, streams, INNER).transpose(0, 2, 1, 3)
    return (
        gated_out.reshape(slab, rows),
        token_grad,
        weight_grad.reshape(256, streams, slab),
        filter_grad,
    )


def solution(mesh):
    placed = (
        P("context", "dp"),
        P(None, None, "dp"),
        P(None, None, "dp"),
        P(("dp", "context"), None),
        P("dp", "context"),
    )
    return jax.shard_map(
        on_device,
        mesh=mesh,
        in_specs=placed,
        out_specs=(
            P("dp", "context"),
            P("context", "dp"),
            P("context", None, "dp"),
            P(("dp", "context"), None),
        ),
        check_vma=False,
    )
```

```python
import functools
import math

import jax
import jax.numpy as jnp
import numpy as np
from jax import lax
from jax.experimental import pallas as pl
from jax.experimental.pallas import tpu as pltpu
from jax.sharding import PartitionSpec as P

OUTER = 64
INNER = 128
TOTAL = OUTER * INNER
HALF = OUTER // 2
KEPT = [0, 8, 16, 24, 32] + [k1 + 8 * k2 for k1 in (1, 2, 3) for k2 in range(8)] + [4, 12, 20, 28]
ROWS = len(KEPT)


def add(a, b):
    return b if a is None else a if b is None else a + b


def neg(a):
    return None if a is None else -a


def sub(a, b):
    return a if b is None else neg(b) if a is None else a - b


def scaled(a, factor):
    if a is None or abs(factor) < 1e-12:
        return None
    if abs(factor - 1) < 1e-12:
        return a
    if abs(factor + 1) < 1e-12:
        return -a
    return a * np.float32(factor)


def cadd(a, b):
    return (add(a[0], b[0]), add(a[1], b[1]))


def csub(a, b):
    return (sub(a[0], b[0]), sub(a[1], b[1]))


def turned(a, step, count):
    step %= count
    if (8 * step) % count == 0 and (8 * step // count) % 2 == 1:
        eighth = 8 * step // count
        root = math.sqrt(0.5)
        re, im = a
        if eighth == 1:
            pair = (sub(re, im), add(re, im))
        elif eighth == 3:
            pair = (neg(add(re, im)), sub(re, im))
        elif eighth == 5:
            pair = (sub(im, re), neg(add(re, im)))
        else:
            pair = (add(re, im), sub(im, re))
        return (scaled(pair[0], root), scaled(pair[1], root))
    angle = 2 * math.pi * step / count
    cos, sin = math.cos(angle), math.sin(angle)
    return (
        sub(scaled(a[0], cos), scaled(a[1], sin)),
        add(scaled(a[0], sin), scaled(a[1], cos)),
    )


def dft(values, sign):
    count = len(values)
    if count == 1:
        return values
    even = dft(values[0::2], sign)
    odd = dft(values[1::2], sign)
    odd = [turned(entry, sign * index, count) for index, entry in enumerate(odd)]
    return [cadd(a, b) for a, b in zip(even, odd)] + [csub(a, b) for a, b in zip(even, odd)]


def outer_forward(load):
    parts = []
    for second in range(8):
        line = [(load(8 * first + second), None) if first < 4 else (None, None) for first in range(8)]
        parts.append(dft(line, -1)[:5])
    results = []
    for first in (0, 1, 2, 3, 4):
        line = [turned(parts[second][first], -second * first, OUTER) for second in range(8)]
        full = dft(line, -1)
        results += {0: full[:5], 4: full[:4]}.get(first, full)
    return results


def real_line(values, count):
    top = values[0][0]
    last = values[4][0]
    a = add(top, last)
    b = sub(top, last)
    (r1, i1), (r2, i2), (r3, i3) = values[1:4]
    s13, d13 = add(r1, r3), sub(r1, r3)
    si, di = add(i1, i3), sub(i1, i3)
    root = math.sqrt(0.5)
    p = scaled(sub(d13, si), root)
    q = scaled(add(d13, si), root)
    out = [
        add(add(a, r2), s13),
        add(sub(b, i2), p),
        sub(sub(a, r2), di),
        sub(add(b, i2), q),
    ]
    if count > 4:
        out += [
            sub(add(a, r2), s13),
            sub(sub(b, i2), p),
            add(sub(a, r2), di),
            add(add(b, i2), q),
        ]
    return out


def outer_inverse(load):
    zero = real_line([load(row) for row in range(5)], 8)
    lines = []
    for first in (1, 2, 3):
        line = dft([load(5 + 8 * (first - 1) + second) for second in range(8)], 1)
        lines.append([turned(line[second], second * first, OUTER) for second in range(8)])
    tail = dft([load(29 + second) if second < 4 else (None, None) for second in range(8)], 1)
    tail = [turned(tail[second], second, 16)[0] for second in range(8)]
    results = [None] * HALF
    for second in range(8):
        line = [(zero[second], None)] + [lines[first][second] for first in range(3)] + [(tail[second], None)]
        for first, entry in enumerate(real_line(line, 4)):
            results[8 * first + second] = entry
    return results


def tables():
    index = np.arange(INNER, dtype=np.float64)
    angle = 2 * np.pi / INNER * (np.outer(index, index) % INNER)
    cos, sin = np.cos(angle), np.sin(angle)
    wide = np.block([[cos, -sin], [sin, cos]])
    high = wide.astype(jnp.bfloat16)
    low = (wide - high.astype(np.float64)).astype(jnp.bfloat16)
    inverse = wide.T
    inverse_high = inverse.astype(jnp.bfloat16)
    inverse_low = (inverse - inverse_high.astype(np.float64)).astype(jnp.bfloat16)
    matrices = np.stack([high, low, inverse_high, inverse_low])
    turn = 2 * np.pi / TOTAL * np.outer(np.array(KEPT, np.float64), index)
    weight = np.array([1.0 if k in (0, HALF) else 2.0 for k in KEPT])[:, None] / TOTAL
    turns = np.stack([np.cos(turn), np.sin(turn), weight * np.cos(turn), weight * np.sin(turn)])
    return matrices, turns.astype(np.float32)


def times_matrix(wide, high, low):
    top = wide.astype(jnp.bfloat16)
    rest = (wide - top.astype(jnp.float32)).astype(jnp.bfloat16)
    dot = functools.partial(jnp.dot, preferred_element_type=jnp.float32)
    return dot(top, high) + (dot(rest, high) + dot(top, low))


def lagged(here, before, lag):
    lane = lax.broadcasted_iota(jnp.int32, here.shape, here.ndim - 1)
    rolled = pltpu.roll(here, lag, here.ndim - 1)
    if before is None:
        return jnp.where(lane < lag, 0.0, rolled)
    return jnp.where(lane < lag, pltpu.roll(before, lag, here.ndim - 1), rolled)


def led(here, after, lead):
    lane = lax.broadcasted_iota(jnp.int32, here.shape, here.ndim - 1)
    width = here.shape[-1]
    rolled = pltpu.roll(here, width - lead, here.ndim - 1)
    if after is None:
        return jnp.where(lane >= width - lead, 0.0, rolled)
    return jnp.where(lane >= width - lead, pltpu.roll(after, width - lead, here.ndim - 1), rolled)


MESH = pl.DeviceIdType.MESH
CHUNK = 512
PIECES = 4


def coords():
    dp = lax.axis_index("dp")
    context = lax.axis_index("context")
    return dp // 2, dp % 2, context // 8, (context // 2) % 4, context % 2


def device(y_hi, core, z, x, y_lo):
    return (y_hi * 2 + core, z * 8 + x * 2 + y_lo)


def greet(partner):
    pl.semaphore_signal(
        pltpu.get_barrier_semaphore(), inc=1, device_id=partner, device_id_type=MESH
    )


def remote(src, dst, send_sem, recv_sem, partner):
    return pltpu.make_async_remote_copy(
        src_ref=src,
        dst_ref=dst,
        send_sem=send_sem,
        recv_sem=recv_sem,
        device_id=partner,
        device_id_type=MESH,
    )


def greet_line():
    dp = lax.axis_index("dp")
    context = lax.axis_index("context")

    @pl.loop(1, 32)
    def _(i):
        greet((dp, lax.rem(context + i, 32)))

    @pl.loop(1, 4)
    def _(i):
        greet((lax.rem(dp + i, 4), context))


def block_kernel(
    tok_ref, cot_ref, filt_hbm, taps_hbm, mat_hbm, turn_hbm, flat_ref,
    gated_hbm, tgrad_hbm, wgrad_hbm, fgrad_hbm,
    filt_ref, mat_ref, turn_ref, taps_all, taps_ref, gated_ref, tgrad_ref, wgrad_ref, wgrad_rows, fgrad_ref, out_sem,
    stage, loose, wide, gathered, outgoing, total, plane, proj, cot,
    fields, spec, prod, gate_ref, gated_group,
    ours, blocks, held, mixed, sums, leaving, arriving, far_out, far_in, own, swap_out, swap_in,
    load_sem, in_sem, pair_sem, half_send, half_recv, pass_send, pass_recv,
    spread_send, spread_recv, plane_sem, proj_send, proj_recv, cot_send, cot_recv,
    back_send, back_recv, gated_send, gated_recv, sib_send, sib_recv, far_sem,
    ring_send, ring_recv, swap_send, swap_recv,
):
    y_hi, core, z, x, y_lo = coords()
    dp = lax.axis_index("dp")
    context = lax.axis_index("context")
    rows, part = tok_ref.shape
    channels = filt_hbm.shape[0]
    size = ROWS * channels
    sibling = device(y_hi, 1 - core, z, x, y_lo)
    opposite = device(1 - y_hi, core, z, x, y_lo)
    slot = z * 4 + x
    chunks = part // CHUNK
    flat_rows = CHUNK * 8

    def quarter(j):
        return 2 * lax.rem(y_hi + j // 2, 2) + lax.rem(core + j % 2, 2)

    def chunk_of(step):
        return quarter(step // chunks) * chunks + step % chunks

    def load(step):
        at = pl.ds(pl.multiple_of(chunk_of(step) * flat_rows, flat_rows), flat_rows)
        return pltpu.make_async_copy(flat_ref.at[at], stage.at[step % 4], load_sem.at[step % 4])

    def cot_copy(i):
        to = lax.rem(context + i, 32)
        return remote(cot_ref.at[to], cot.at[context], cot_send.at[i], cot_recv.at[i], (dp, to))

    def separate(first, last, sends=False):
        @pl.loop(first, last)
        def _(step):
            load(step).wait()
            loose[...] = stage[step % 4].astype(jnp.float32)
            at = pl.ds(pl.multiple_of(chunk_of(step) * CHUNK, CHUNK), CHUNK)
            for stream in range(2):
                for tile in range(4):
                    column = stream * 512 + tile * INNER
                    wide[at, column : column + INNER] = loose[
                        pl.ds(2 * tile + stream, CHUNK, stride=8), :
                    ].astype(jnp.bfloat16)

            @pl.when(step + 4 < 4 * chunks)
            def _():
                load(step + 4).start()

            for j in range(4 if sends else 0):
                to = 1 + (step - first) * 4 + j

                @pl.when(to < 32)
                def _():
                    cot_copy(to).start()

    def multiply(j, first, last):
        for piece in range(first, last):
            at = pl.ds(pl.multiple_of((quarter(j) * chunks + piece) * CHUNK, CHUNK), CHUNK)
            total[...] += jnp.dot(
                gathered[quarter(j), :, piece * CHUNK : (piece + 1) * CHUNK],
                wide[at, :],
                preferred_element_type=jnp.float32,
            )

    own_tokens = pltpu.make_async_copy(tok_ref, gathered.at[dp], in_sem.at[0])
    own_cot = pltpu.make_async_copy(cot_ref.at[context], cot.at[context], in_sem.at[1])
    own_tables = [
        pltpu.make_async_copy(src, dst, in_sem.at[2 + i])
        for i, (src, dst) in enumerate(((filt_hbm, filt_ref), (mat_hbm, mat_ref), (turn_hbm, turn_ref), (taps_hbm, taps_all)))
    ]
    for step in range(4):
        load(step).start()
    own_tokens.start()
    own_cot.start()
    for copy in own_tables:
        copy.start()
    greet_line()

    @pl.loop(1, 16)
    def _(i):
        other = lax.rem(slot + i, 16)
        greet(device(y_hi, 1 - core, other // 4, other % 4, y_lo))

    pl.semaphore_wait(pltpu.get_barrier_semaphore(), 34 + 15)

    width = part // PIECES
    pieces = [
        remote(
            tok_ref.at[:, i * width : (i + 1) * width],
            gathered.at[dp, :, i * width : (i + 1) * width],
            half_send.at[i], half_recv.at[i], opposite,
        )
        for i in range(PIECES)
    ]
    token_pair = remote(tok_ref, gathered.at[dp], pair_sem.at[0], pair_sem.at[1], sibling)
    pieces[0].start()
    token_pair.start()
    for copy in pieces[1:]:
        copy.start()
    own_tokens.wait()
    far = 2 * (1 - y_hi) + core
    passed = [
        remote(
            gathered.at[far, :, i * width : (i + 1) * width],
            gathered.at[far, :, i * width : (i + 1) * width],
            pass_send.at[i], pass_recv.at[i], sibling,
        )
        for i in range(PIECES)
    ]

    def spread(which, i, block):
        to_x = i // 2
        to_core = i % 2
        column = pl.multiple_of(512 * to_x + 256 * to_core, 256)
        src = gathered.at[block, :, pl.ds(column, 256)]
        here = (block == z) & (to_x == x) & (to_core == core)
        there = remote(
            src, plane.at[to_core, slot], spread_send.at[which * 8 + i], spread_recv.at[slot],
            device(y_hi, to_core, block, to_x, y_lo),
        )
        return here, there, src

    def spread_start(which, block, first, last):
        @pl.loop(first, last)
        def _(i):
            here, there, src = spread(which, i, block)

            @pl.when(here)
            def _():
                pltpu.make_async_copy(src, plane.at[core, slot], spread_recv.at[slot]).start()

            @pl.when(jnp.logical_not(here))
            def _():
                there.start()

    def spread_done(which, block):
        @pl.loop(0, 8)
        def _(i):
            here, there, _src = spread(which, i, block)

            @pl.when(jnp.logical_not(here))
            def _():
                there.wait_send()

    across = device(y_hi, core, z, x, 1 - y_lo)
    plane_pair = remote(plane.at[core], plane.at[core], plane_sem.at[0], plane_sem.at[1], sibling)

    spread_start(0, dp, 0, 8)

    total[...] = jnp.zeros_like(total)
    separate(0, 3)
    separate(3, 11, True)
    multiply(0, 0, 4)
    token_pair.wait_recv()
    for i in range(PIECES):
        if i < 3:
            pieces[i].wait_recv()
            passed[i].start()
            spread_start(1, far, 2 * i, 2 * i + 2)
            separate(11 + i, 12 + i)
        else:
            separate(14, 16)
            multiply(1, 0, 4)
            multiply(2, 0, 3)
            for n in range(3):
                passed[n].wait_recv()
                multiply(3, n, n + 1)
            pieces[i].wait_recv()
            passed[i].start()
            multiply(2, 3, 4)
            passed[3].wait_recv()
            multiply(3, 3, 4)
    def transform(begin, end):
        @pl.loop(begin, end)
        def _(which):
            for row, (re, im) in enumerate(outer_forward(lambda n: fields[which, n])):
                cos = turn_ref[0, row][None, :]
                sin = turn_ref[1, row][None, :]
                at = pl.ds(row * channels, channels)
                if im is None:
                    spec[which, at, :INNER] = re * cos
                    spec[which, at, INNER:] = -(re * sin)
                else:
                    spec[which, at, :INNER] = re * cos + im * sin
                    spec[which, at, INNER:] = im * cos - re * sin
            spec[which] = times_matrix(spec[which], mat_ref[0], mat_ref[1])

    outgoing[...] = total[...].T.astype(jnp.bfloat16).reshape(outgoing.shape)

    def proj_copy(i):
        to = lax.rem(context + i, 32)
        return remote(outgoing.at[:, to], proj.at[context], proj_send.at[i], proj_recv.at[i], (dp, to))

    @pl.loop(1, 32)
    def _(i):
        proj_copy(i).start()

    proj[context] = outgoing[:, context]
    spread_start(1, far, 6, 8)
    for copy in own_tables:
        copy.wait()

    tile = pl.ds(pl.multiple_of(context // 8 * INNER, INNER), INNER)
    lane = lax.broadcasted_iota(jnp.int32, (channels, INNER), 1)
    picked = lane == context % 8 * channels + lax.broadcasted_iota(jnp.int32, (channels, INNER), 0)
    for stream in range(2):
        for lag in range(3):
            line = taps_all[lag, pl.ds(stream, 1), tile]
            column = jnp.sum(jnp.where(picked, line, 0.0), axis=1, keepdims=True)
            taps_ref[stream, lag] = jnp.broadcast_to(column, (channels, INNER))
    for n in range(HALF):
        fields[0, n] = filt_ref[:, n * INNER : (n + 1) * INNER]

    @pl.loop(1, 32)
    def _(i):
        cot_copy(i).wait_recv()

    own_cot.wait()

    @pl.loop(1, 32)
    def _(i):
        proj_copy(i).wait_recv()

    def short(stream, n):
        here = proj[n, stream].astype(jnp.float32)
        before = proj[n - 1, stream].astype(jnp.float32) if n else None
        result = taps_ref[stream, 0] * here
        for lag in (1, 2):
            result = result + taps_ref[stream, lag] * lagged(here, before, lag)
        return result

    for n in range(HALF):
        gate = short(0, n)
        gate_ref[n] = gate
        fields[2, n] = cot[n].astype(jnp.float32) * gate
        fields[1, n] = short(1, n)

    transform(0, 3)

    @pl.loop(0, ROWS)
    def _(row):
        at = pl.ds(pl.multiple_of(row * channels, channels), channels)
        (hr, hi), (vr, vi), (gr, gi) = [
            (spec[which, at, :INNER], spec[which, at, INNER:]) for which in range(3)
        ]

        def put(which, re, im):
            prod[which, at, :INNER] = re
            prod[which, at, INNER:] = im

        put(0, hr * vr - hi * vi, hr * vi + hi * vr)
        put(1, hr * gr + hi * gi, hr * gi - hi * gr)
        put(2, vr * gr + vi * gi, vr * gi - vi * gr)

    @pl.loop(0, 3)
    def _(which):
        prod[which] = times_matrix(prod[which], mat_ref[2], mat_ref[3])

        def turned_row(row):
            cos = turn_ref[2, row][None, :]
            sin = turn_ref[3, row][None, :]
            at = pl.ds(row * channels, channels)
            re, im = prod[which, at, :INNER], prod[which, at, INNER:]
            return re * cos - im * sin, im * cos + re * sin

        for n, entry in enumerate(outer_inverse(turned_row)):
            fields[which, n] = entry

    for n in range(HALF):
        entry = fields[0, n]
        gated_group[n] = (gate_ref[n] * entry).astype(jnp.bfloat16)
        gate_ref[n] = cot[n].astype(jnp.float32) * entry

    for stream, load_row in enumerate((lambda n: gate_ref[n], lambda n: fields[1, n])):
        for n in range(HALF):
            here = load_row(n)
            after = load_row(n + 1) if n + 1 < HALF else None
            result = taps_ref[stream, 0] * here
            for lead in (1, 2):
                result = result + taps_ref[stream, lead] * led(here, after, lead)
            column = n // 2 * INNER
            ours[stream, n % 2, :, column : column + INNER] = result.astype(jnp.bfloat16)

    def group_rows(group):
        return pl.ds(pl.multiple_of(group * channels, channels), channels)

    def column_of(index):
        return pl.ds(pl.multiple_of(index // 2 * INNER, INNER), INNER)

    def back_copy(i):
        to = lax.rem(context + i, 32)
        return remote(
            ours.at[:, to % 2, :, column_of(to)], held.at[:, group_rows(context)],
            back_send.at[i], back_recv.at[i], (dp, to),
        )

    def back_arrival(i):
        source = lax.rem(context + 32 - i, 32)
        return remote(
            ours.at[:, source % 2, :, column_of(source)], held.at[:, group_rows(source)],
            back_send.at[i], back_recv.at[i], (dp, source),
        )

    ours_across = remote(
        ours.at[:, 1 - y_lo], blocks.at[:, slot, y_lo], plane_sem.at[2], plane_sem.at[3], across
    )

    def gated_copy(i):
        to = lax.rem(context + i, 32)
        return remote(
            gated_group.at[to], gated_ref.at[context], gated_send.at[i], gated_recv.at[i], (dp, to)
        )

    def leave(which):
        src, dst = (
            (gated_ref, gated_hbm), (tgrad_ref, tgrad_hbm), (wgrad_ref, wgrad_hbm), (fgrad_ref, fgrad_hbm),
        )[which]
        return pltpu.make_async_copy(src, dst, out_sem.at[which])

    @pl.loop(1, 32)
    def _(i):
        back_copy(i).start()

    ours_across.start()
    blocks[:, slot, y_lo] = ours[:, y_lo]

    def place(first, along, aside):
        if first == "x":
            return lax.rem(z + aside + 4, 4) * 4 + lax.rem(x + along + 4, 4)
        return lax.rem(z + along + 4, 4) * 4 + lax.rem(x + aside + 4, 4)

    def neighbour(first, along, aside):
        at = place(first, along, aside)
        return device(y_hi, core, at // 4, at % 4, y_lo)

    class Unit:
        def __init__(self, number):
            self.stream = number // 2
            self.from_y = (y_lo, 1 - y_lo)[number % 2]
            self.first = ("x", "z")[number % 2]
            self.base = 20 * number
            self.started = []

        def copy(self, index, along, aside, part, step_along, step_aside):
            begin, count = {None: (0, 2048), 0: (0, 1024), 1: (1024, 1024)}[part]
            ref = blocks.at[
                self.stream,
                place(self.first, along, aside),
                self.from_y,
                :,
                pl.ds(begin, count),
            ]
            return remote(
                ref, ref, ring_send.at[self.base + index], ring_recv.at[self.base + index],
                neighbour(self.first, step_along, step_aside),
            )

        def send(self, *args):
            copy = self.copy(*args)
            copy.start()
            self.started.append(copy)

        def arrived(self, index, along, aside, part):
            self.copy(index, along, aside, part, 1, 0).wait_recv()

        def send_line(self, which, along):
            self.send(4 + 4 * which, along, 0, None, 0, 1)
            self.send(5 + 4 * which, along, 0, None, 0, -1)

        def pass_line(self, which, along):
            self.arrived(4 + 4 * which, along, -1, None)
            self.send(6 + 4 * which, along, -1, 0, 0, 1)
            self.arrived(5 + 4 * which, along, 1, None)
            self.send(7 + 4 * which, along, 1, 1, 0, -1)

        def begin(self):
            self.send(0, 0, 0, None, 1, 0)
            self.send(1, 0, 0, None, -1, 0)

        def relay(self):
            self.arrived(0, -1, 0, None)
            self.send(2, -1, 0, 0, 1, 0)
            self.arrived(1, 1, 0, None)
            self.send(3, 1, 0, 1, -1, 0)

        def lines(self):
            self.send_line(1, -1)
            self.send_line(2, 1)

        def last_line(self):
            self.arrived(2, -2, 0, 0)
            self.arrived(3, 2, 0, 1)
            self.send_line(3, 2)

        def end(self):
            for which, along in enumerate((0, -1, 1, 2)):
                self.arrived(6 + 4 * which, along, -2, 0)
                self.arrived(7 + 4 * which, along, 2, 1)

    units = [Unit(number) for number in range(4)]

    def weight_copy(which):
        return remote(
            swap_out.at[which], swap_in.at[which], swap_send.at[which], swap_recv.at[which], across
        )

    def weight_sum(which, half):
        return jnp.dot(
            blocks[which // 2, :, (y_lo, 1 - y_lo)[which % 2]].reshape(256, 16 * INNER),
            plane[half].reshape(16 * INNER, 256),
            preferred_element_type=jnp.float32,
        )

    def weight_send(which):
        swap_out[which] = weight_sum(which, 1 - y_lo).astype(jnp.bfloat16)
        weight_copy(which).start()

    def weight_own(which):
        sums[which] = weight_sum(which, y_lo)

    def weight_end(stream):
        for mine, theirs in ((2 * stream + 1, 2 * stream), (2 * stream, 2 * stream + 1)):
            weight_copy(theirs).wait_recv()
            value = sums[mine] + swap_in[theirs].astype(jnp.float32)
            mixed[:, (y_lo, 1 - y_lo)[mine % 2]] = value.reshape(16, channels, 256)
        turned_sum = mixed[...].reshape(512, 256).T
        for tile in range(4):
            wgrad_rows[pl.ds(2 * tile + stream, 256, stride=8), :] = turned_sum[
                :, tile * INNER : (tile + 1) * INNER
            ]

    def product(q, put, first, last):
        shard = held[...].reshape(1024, INNER)
        for i in range(first, last):
            at = pl.ds(pl.multiple_of(q * part + i * CHUNK, CHUNK), CHUNK)
            put(
                pl.ds(i * CHUNK, CHUNK),
                jnp.dot(wide[at, :], shard, preferred_element_type=jnp.float32),
            )

    def chunk_rows(i):
        return pl.ds(i * CHUNK, CHUNK)

    def to_sibling(which, i):
        at = chunk_rows(i)
        return remote(
            leaving.at[which, at], arriving.at[which, at],
            sib_send.at[4 * which + i], sib_recv.at[4 * which + i], sibling,
        )

    def for_sibling(which, y):
        def put(at, value):
            leaving[which, at, :] = value.astype(jnp.bfloat16)

        for i in range(chunks):
            product(2 * y + 1 - core, put, i, i + 1)
            to_sibling(which, i).start()

    def keep(which, y, i):
        def put(at, value):
            own[at, :] = value

        product(2 * y + core, put, i, i + 1)
        to_sibling(which, i).wait_recv()

    def far_copy(i):
        at = chunk_rows(i)
        return remote(far_out.at[at], far_in.at[at], far_sem.at[i], far_sem.at[4 + i], opposite)

    units[0].begin()
    units[2].begin()
    units[0].send_line(0, 0)
    held[:, group_rows(context)] = ours[:, y_lo, :, column_of(context)]
    gated_ref[context] = gated_group[context]
    for n in range(HALF):
        fgrad_ref[:, n * INNER : (n + 1) * INNER] = fields[2, n]
    leave(3).start()

    @pl.loop(0, 16)
    def _(i):
        ref = plane.at[core, i]
        remote(ref, ref, spread_send.at[0], spread_recv.at[i], sibling).wait_recv()

    plane_pair.start()
    ours_across.wait_recv()
    units[1].begin()
    units[3].begin()
    for unit in units[1:]:
        unit.send_line(0, 0)
    for unit in units[:2]:
        unit.relay()
        unit.lines()
    for unit in units[2:]:
        unit.relay()

    @pl.loop(1, 32)
    def _(i):
        back_arrival(i).wait_recv()

    for_sibling(0, 1 - y_hi)
    for unit in units[:2]:
        unit.pass_line(0, 0)
        unit.last_line()
    for i in range(chunks):
        keep(0, 1 - y_hi, i)
        at = chunk_rows(i)
        far_out[at, :] = (own[at, :] + arriving[0, at, :].astype(jnp.float32)).astype(jnp.bfloat16)
        far_copy(i).start()
    for unit in units[2:]:
        unit.lines()
    for unit in units[:2]:
        unit.pass_line(1, -1)
        unit.pass_line(2, 1)
    for unit in units[2:]:
        unit.pass_line(0, 0)
        unit.last_line()
    for unit in units[:2]:
        unit.pass_line(3, 2)

    @pl.loop(1, 32)
    def _(i):
        gated_copy(i).start()

    for unit in units[2:]:
        unit.pass_line(1, -1)
        unit.pass_line(2, 1)
    for_sibling(1, y_hi)
    for unit in units[2:]:
        unit.pass_line(3, 2)
    plane_pair.wait_recv()
    for i in range(4):
        units[i].end()
        weight_send(i)
    for i in range(chunks):
        keep(1, y_hi, i)
        at = chunk_rows(i)
        own[at, :] += arriving[1, at, :].astype(jnp.float32)

    @pl.loop(1, 32)
    def _(i):
        cot_copy(i).wait_send()
        proj_copy(i).wait_send()
        back_copy(i).wait_send()
        gated_copy(i).wait()

    leave(0).start()
    for copy in pieces + passed + [token_pair, plane_pair, ours_across]:
        copy.wait_send()
    spread_done(0, dp)
    spread_done(1, far)
    for i in range(4):
        weight_own(i)
    weight_end(0)
    for i in range(chunks):
        far_copy(i).wait_recv()
        at = chunk_rows(i)
        tgrad_ref[:, i * CHUNK : (i + 1) * CHUNK] = (
            (own[at, :] + far_in[at, :].astype(jnp.float32)).T.astype(jnp.bfloat16)
        )
    leave(1).start()
    for unit in units:
        for copy in unit.started:
            copy.wait_send()
    for i in range(chunks):
        far_copy(i).wait_send()
        for which in range(2):
            to_sibling(which, i).wait_send()
    for i in range(4):
        weight_copy(i).wait_send()
    weight_end(1)
    wgrad_ref[...] = wgrad_rows[...].astype(jnp.bfloat16)
    leave(2).start()
    for i in range(4):
        leave(i).wait()


def finish_kernel(*refs):
    sources, targets, held, sem = refs[:4], refs[4:8], refs[8:12], refs[12]
    arrive = [pltpu.make_async_copy(a, b, sem.at[i]) for i, (a, b) in enumerate(zip(sources, held))]
    depart = [pltpu.make_async_copy(a, b, sem.at[4 + i]) for i, (a, b) in enumerate(zip(held, targets))]
    for copy in arrive:
        copy.start()
    for first, second in zip(arrive, depart):
        first.wait()
        second.start()
    for copy in depart:
        copy.wait()


def finished(*arrays):
    hbm = pl.BlockSpec(memory_space=pl.ANY)
    return pl.pallas_call(
        finish_kernel,
        out_shape=tuple(jax.ShapeDtypeStruct(array.shape, array.dtype) for array in arrays),
        in_specs=[hbm] * 4,
        out_specs=[hbm] * 4,
        scratch_shapes=[pltpu.VMEM(array.shape, array.dtype) for array in arrays]
        + [pltpu.SemaphoreType.DMA((8,))],
        compiler_params=pltpu.CompilerParams(vmem_limit_bytes=56 * 1024 * 1024),
        name="results",
    )(*arrays)


def on_device(tokens, in_weight, short_taps, filters, cotangent):
    channels, length = filters.shape
    groups = lax.axis_size("context")
    rows, part = tokens.shape
    depth, streams, slab = in_weight.shape
    tiles = slab // INNER
    flat = (
        in_weight.reshape(depth, streams, tiles, INNER)
        .transpose(0, 2, 1, 3)
        .reshape(depth * streams * tiles, INNER)
    )
    matrices, turns = tables()
    hbm = pl.BlockSpec(memory_space=pl.ANY)

    def bf16(*shape):
        return pltpu.VMEM(shape, jnp.bfloat16)

    def f32(*shape):
        return pltpu.VMEM(shape, jnp.float32)

    def dma(*counts):
        return [pltpu.SemaphoreType.DMA((count,)) for count in counts]

    size = ROWS * channels
    results = pl.pallas_call(
        block_kernel,
        out_shape=(
            jax.ShapeDtypeStruct((groups, channels, rows), jnp.bfloat16),
            jax.ShapeDtypeStruct((rows, part), jnp.bfloat16),
            jax.ShapeDtypeStruct((256 * streams * tiles, INNER), jnp.bfloat16),
            jax.ShapeDtypeStruct((channels, length), jnp.float32),
        ),
        in_specs=[hbm] * 7,
        out_specs=[hbm] * 4,
        scratch_shapes=[
            f32(channels, length),
            bf16(*matrices.shape),
            f32(*turns.shape),
            f32(3, streams, slab),
            f32(streams, 3, channels, INNER),
            bf16(groups, channels, rows),
            bf16(rows, part),
            bf16(256 * streams * tiles, INNER),
            f32(256 * streams * tiles, INNER),
            f32(channels, length),
            *dma(4),
            bf16(4, CHUNK * 8, INNER),
            f32(CHUNK * 8, INNER),
            bf16(depth, streams * slab),
            bf16(4, rows, part),
            bf16(streams, groups, channels, rows),
            f32(rows, streams * slab),
            bf16(2, 16, rows, 256),
            bf16(groups, streams, channels, rows),
            bf16(groups, channels, rows),
            f32(3, HALF, channels, INNER),
            f32(3, size, 2 * INNER),
            f32(3, size, 2 * INNER),
            f32(HALF, channels, INNER),
            bf16(groups, channels, rows),
            bf16(streams, 2, channels, length // 2),
            bf16(streams, 16, 2, channels, length // 2),
            bf16(streams, slab, rows),
            f32(16, 2, channels, 256),
            f32(4, slab // 2, 256),
            bf16(2, part, rows),
            bf16(2, part, rows),
            bf16(part, rows),
            bf16(part, rows),
            f32(part, rows),
            bf16(4, slab // 2, 256),
            bf16(4, slab // 2, 256),
            *dma(4, 6, 2, PIECES, PIECES, PIECES, PIECES, 16, 16, 4, 32, 32, 32, 32),
            *dma(32, 32, 32, 32, 8, 8, 8, 80, 80, 4, 4),
        ],
        compiler_params=pltpu.CompilerParams(
            collective_id=0, has_side_effects=True, vmem_limit_bytes=56 * 1024 * 1024
        ),
        cost_estimate=pl.CostEstimate(
            flops=8_000_000_000, bytes_accessed=24_000_000, transcendentals=0
        ),
        name="block_forward_backward",
    )(
        tokens, cotangent.reshape(groups, channels, rows), filters, short_taps.transpose(1, 0, 2),
        jnp.asarray(matrices), jnp.asarray(turns), flat,
    )
    gated_out, token_grad, weight_grad, filter_grad = finished(*results)
    weight_grad = weight_grad.reshape(256, tiles, streams, INNER).transpose(0, 2, 1, 3)
    return (
        gated_out.reshape(slab, rows),
        token_grad,
        weight_grad.reshape(256, streams, slab),
        filter_grad,
    )


def solution(mesh):
    placed = (
        P("context", "dp"),
        P(None, None, "dp"),
        P(None, None, "dp"),
        P(("dp", "context"), None),
        P("dp", "context"),
    )
    return jax.shard_map(
        on_device,
        mesh=mesh,
        in_specs=placed,
        out_specs=(
            P("dp", "context"),
            P("context", "dp"),
            P("context", None, "dp"),
            P(("dp", "context"), None),
        ),
        check_vma=False,
    )
```
